32 devices in a mesh: dom: 8 (over z, y), serve: 4 (over x, core).
Axes of the slice: x: 2, y: 2, z: 4, core: 2. Of those that a mesh axis runs over, the one named last changes fastest.
Arguments:
- source_rows: float32 [8, 4, 256, 400], P('dom', 'serve'), may hold values from -1.5 to 1.5
- source_state: float32 [8, 4, 256], P('dom', 'serve'), may hold values from 0.01 to 1
- target_rows: float32 [8, 4, 256, 400], P('dom', 'serve'), may hold values from -1.5 to 1.5
- target_state: float32 [8, 4, 256], P('dom', 'serve'), may hold values from 0.01 to 1
- relation_table: float32 [16, 400], replicated, may hold values from -4 to 4
- source_ids: int32 [8, 4, 2, 8, 128], P('dom', 'serve'), may hold values from 0 to 255
- target_ids: int32 [8, 4, 2, 8, 128], P('dom', 'serve'), may hold values from 0 to 255
- relation_ids: int32 [8, 4, 2, 8, 128], P('dom', 'serve'), may hold values from 0 to 15
- negative_block: int32 [8, 4, 2, 8], P('dom', 'serve'), may hold values from 0 to 1
- edge_counts: int32 [8, 4, 2, 8], P('dom', 'serve'), may hold values from 1 to 128, 768 in all within a row
- serving_shard: int32 [8, 4, 256], P('dom', 'serve'), may hold values from 0 to 3
- changed_rows: int32 [8, 4, 256], P('dom', 'serve'), may hold values from 0 to 1, as said below
Outputs:
- new_source: float32 [8, 4, 256, 400], P('dom', 'serve')
- new_source_state: float32 [8, 4, 256], P('dom', 'serve')
- new_target: float32 [8, 4, 256, 400], P('dom', 'serve')
- new_target_state: float32 [8, 4, 256], P('dom', 'serve')
- served: bfloat16 [8, 4, 4, 256, 400], P('dom', 'serve')
The draws below stay inside these ranges and needn't reach their ends.
Inputs may be any that keep to these rules, and one draw needn't show every extreme that they name: `edge_counts`: for one device and step, the 8 counts sum to 768 and the largest is exactly 128. `changed_rows`: on every device at most 64 changed rows have one serving shard, and exactly 64 have some shard, the same shard for all devices of one index of dom.
All inputs are finite; a program needn't handle non-finite values.
Results may differ from the reference program's by a relative error of at most 0.001.
Values may be sent and summed in bfloat16 or wider, within the bound.
A program may use at most 64 MiB of HBM per device.

```python
import math
import jax
import jax.numpy as jnp
import numpy as np
from jax import lax

D = 400
NREL = 16
EDGE_BLOCK = 128
STEPS = 2
ROWS = 256
NB = 8
PARTITIONS = 8
SHARDS = 4


def serving_plan(key):
    base = jax.random.fold_in(key, 7)
    perm_key, order_key, count_key = jax.random.split(base, 3)
    devices_count = PARTITIONS * SHARDS
    row_perms = jax.vmap(lambda single: jax.random.permutation(single, ROWS))(jax.random.split(perm_key, devices_count))
    position = jnp.argsort(row_perms, axis=1).astype(jnp.int32)
    segment = (position >= ROWS // 2).astype(jnp.int32) + (position >= 3 * ROWS // 4).astype(jnp.int32) + (position >= 7 * ROWS // 8).astype(jnp.int32)
    starts = jnp.array([0, ROWS // 2, 3 * ROWS // 4, 7 * ROWS // 8], jnp.int32)
    orders = jax.vmap(lambda single: jax.random.permutation(single, 4))(jax.random.split(order_key, PARTITIONS)).astype(jnp.int32)
    orders = jnp.repeat(orders, SHARDS, axis=0)
    shard_of_row = jnp.take_along_axis(orders, segment, axis=1)
    upper = jnp.array([ROWS // 4, ROWS // 8, ROWS // 8], jnp.int32)
    others = jax.random.randint(count_key, (devices_count, 3), 1, upper[None, :] + 1).astype(jnp.int32)
    limits = jnp.concatenate([jnp.full((devices_count, 1), ROWS // 4, jnp.int32), others], axis=1)
    offset = position - starts[segment]
    chosen = (offset < jnp.take_along_axis(limits, segment, axis=1)).astype(jnp.int32)
    return (shard_of_row.reshape(PARTITIONS, SHARDS, ROWS), chosen.reshape(PARTITIONS, SHARDS, ROWS))


def draw_serving_shard(key, part):
    return serving_plan(key)[0]


def draw_changed_rows(key, part):
    return serving_plan(key)[1]


def place_ends(values, stream_key, low, largest):
    extent = values.shape
    place = [jax.random.randint(jax.random.fold_in(stream_key, axis), (), 0, extent[axis]) for axis in range(len(extent))]
    values = values.at[tuple(place)].set(low)
    longest = extent.index(max(extent))
    place[longest] = (place[longest] + 1) % extent[longest]
    return values.at[tuple(place)].set(largest)


def steps_of(key, extent, cuts, smallest, high):
    def one(axis_at, shards_of):
        heights = jax.random.uniform(jax.random.fold_in(jax.random.fold_in(key, 6), axis_at), (shards_of,), jnp.float32, smallest / len(cuts), high / len(cuts))
        return jnp.repeat(jnp.exp(heights), extent[axis_at] // shards_of).reshape((-1,) + (1,) * (len(extent) - axis_at - 1))

    level = one(*cuts[0])
    for cut in cuts[1:]:
        level = level * one(*cut)
    return level


def split_up(number_of, total, bound, lean):
    loads = [(1 << 20) // math.isqrt(rank ** lean) + 1 for rank in range(2, number_of + 1)]
    surplus, given = total - bound - (number_of - 1), [1] * (number_of - 1)
    while surplus > 0:
        free = [i for i in range(number_of - 1) if given[i] < bound]
        whole, remaining = sum([loads[i] for i in free]), surplus
        for i in free:
            extra = min(bound - given[i], max(1, remaining * loads[i] // whole), surplus)
            given[i] = given[i] + extra
            surplus = surplus - extra
    return np.array([bound] + given)


def uneven_parts(stream_key, number_of, total, reach, skew):
    if number_of == 2:
        one = jax.random.randint(stream_key, (), max(1, total - reach), min(reach, total - 1) + 1)
        return jnp.stack([one, total - one])
    lengths = jnp.asarray(split_up(number_of, total, reach, skew), jnp.int32)
    twos = (number_of - 1) // 2
    giver, taker = lengths[1:1 + 2 * twos:2], lengths[2:2 + 2 * twos:2]
    slack = jnp.minimum(giver - 1, reach - taker)
    moved = jax.random.randint(jax.random.fold_in(stream_key, 1), (twos,), 0, 1 << 20) % (slack + 1)
    lengths = lengths.at[1:1 + 2 * twos:2].set(giver - moved).at[2:2 + 2 * twos:2].set(taker + moved)
    return lengths[jax.random.permutation(jax.random.fold_in(stream_key, 2), number_of)]


def noise(stream_key, extent, deviation, most, cuts=(), kind=jnp.bfloat16):
    values = deviation * jax.random.normal(stream_key, extent, jnp.float32)
    if cuts:
        values = values * steps_of(stream_key, extent, cuts, -0.22, 0.18)
    return jnp.clip(values, -most, most).astype(kind)


def setup_inputs(seed: int = 0) -> dict:
    seeds = jax.random.split(jax.random.key(seed), 13)
    source_rows = noise(seeds[0], (PARTITIONS, SHARDS, ROWS, D), 0.25, 1.5, ((0, 8), (1, 4)), jnp.float32)
    source_state = jnp.clip(jnp.exp(math.log(1.0) - 4.6051702 * jax.random.uniform(seeds[1], (PARTITIONS, SHARDS, ROWS), jnp.float32) ** steps_of(seeds[1], (PARTITIONS, SHARDS, ROWS), ((0, 8), (1, 4)), -0.2, 0.2)), 0.01, 1.0)
    target_rows = noise(seeds[2], (PARTITIONS, SHARDS, ROWS, D), 0.25, 1.5, ((0, 8), (1, 4)), jnp.float32)
    target_state = jnp.clip(jnp.exp(math.log(1.0) - 4.6051702 * jax.random.uniform(seeds[3], (PARTITIONS, SHARDS, ROWS), jnp.float32) ** steps_of(seeds[3], (PARTITIONS, SHARDS, ROWS), ((0, 8), (1, 4)), -0.2, 0.2)), 0.01, 1.0)
    relation_table = noise(seeds[4], (NREL, D), 1.0, 4.0, (), jnp.float32)
    source_ids = place_ends(jax.random.randint(seeds[5], (PARTITIONS, SHARDS, STEPS, NB, EDGE_BLOCK), 0, ROWS), jax.random.fold_in(seeds[5], 1), 0, ROWS - 1).astype(jnp.int32)
    target_ids = place_ends(jax.random.randint(seeds[6], (PARTITIONS, SHARDS, STEPS, NB, EDGE_BLOCK), 0, ROWS), jax.random.fold_in(seeds[6], 1), 0, ROWS - 1).astype(jnp.int32)
    relation_ids = place_ends(jax.random.randint(seeds[7], (PARTITIONS, SHARDS, STEPS, NB, EDGE_BLOCK), 0, NREL), jax.random.fold_in(seeds[7], 1), 0, NREL - 1).astype(jnp.int32)
    negative_block = place_ends(jax.random.randint(seeds[8], (PARTITIONS, SHARDS, STEPS, NB), 0, ROWS // 128), jax.random.fold_in(seeds[8], 1), 0, (ROWS // 128) - 1).astype(jnp.int32)
    edge_counts = jax.vmap(lambda own: uneven_parts(own, NB, 96 * NB, EDGE_BLOCK, 2))(jax.random.split(seeds[9], PARTITIONS * SHARDS * STEPS)).reshape((PARTITIONS, SHARDS, STEPS, NB)).astype(jnp.int32)
    serving_shard = draw_serving_shard(jax.random.fold_in(seeds[12], 71), 0)
    changed_rows = draw_changed_rows(jax.random.fold_in(seeds[12], 71), 0)
    return dict(source_rows=source_rows, source_state=source_state, target_rows=target_rows, target_state=target_state, relation_table=relation_table, source_ids=source_ids, target_ids=target_ids, relation_ids=relation_ids, negative_block=negative_block, edge_counts=edge_counts, serving_shard=serving_shard, changed_rows=changed_rows)


HIGHEST_PRECISION = lax.Precision.HIGHEST
LEARN_RATE = 0.1
EPSILON = 1e-08

def adagrad_update(weights, state, gradient):
    new_state = state + lax.optimization_barrier(jnp.mean(gradient * gradient, axis=-1))
    return (weights - LEARN_RATE * gradient / (jnp.sqrt(new_state)[:, None] + EPSILON), new_state)

def train_bucket(source, source_sums, target, target_sums, edge_source, edge_target, edge_relation, negative_ids, counts, relation_table):
    blocks, lanes_count = edge_source.shape
    row_count, width = source.shape
    relation_count = relation_table.shape[0]
    per_group = min(8, blocks)
    lane_ids = jnp.arange(lanes_count, dtype=jnp.int32)
    grad_source = jnp.zeros((row_count, width), source.dtype)
    grad_target = jnp.zeros((row_count, width), source.dtype)
    for block_start in range(0, blocks, per_group):
        source_idx = edge_source[block_start:block_start + per_group]
        target_idx = edge_target[block_start:block_start + per_group]
        relation_idx = edge_relation[block_start:block_start + per_group]
        negative_idx = negative_ids[block_start:block_start + per_group][:, None] * lanes_count + lane_ids[None, :]
        source_part = source[source_idx]
        target_part = target[target_idx]
        negative_part = target[negative_idx]
        selector = (relation_idx.reshape(-1)[:, None] == jnp.arange(relation_count, dtype=jnp.int32)[None, :]).astype(source.dtype)
        relation_part = jnp.dot(selector, relation_table, precision=HIGHEST_PRECISION).reshape(per_group, lanes_count, width)
        query = source_part * relation_part
        positive = lax.optimization_barrier(jnp.sum(query * target_part, axis=-1))
        negative = jnp.einsum('gid,gjd->gij', query, negative_part, precision=HIGHEST_PRECISION)
        valid = (lane_ids[None, :] < counts[block_start:block_start + per_group][:, None]).astype(source.dtype)
        positive_grad = -jax.nn.sigmoid(-positive) * valid
        negative_grad = jax.nn.sigmoid(negative) * (valid[:, :, None] / lanes_count)
        query_grad = positive_grad[..., None] * target_part + jnp.einsum('gij,gjd->gid', negative_grad, negative_part, precision=HIGHEST_PRECISION)
        grad_source = grad_source.at[source_idx.reshape(-1)].add((query_grad * relation_part).reshape(-1, width))
        grad_target = grad_target.at[target_idx.reshape(-1)].add((positive_grad[..., None] * query).reshape(-1, width))
        negative_term = jnp.einsum('gij,gid->gjd', negative_grad, query, precision=HIGHEST_PRECISION)
        grad_target = grad_target.at[negative_idx.reshape(-1)].add(negative_term.reshape(-1, width))
    source, source_sums = adagrad_update(source, source_sums, grad_source)
    target, target_sums = adagrad_update(target, target_sums, grad_target)
    return (source, source_sums, target, target_sums)

def reference(source_rows, source_state, target_rows, target_state, relation_table, source_ids, target_ids, relation_ids, negative_block, edge_counts, serving_shard, changed_rows):
    parts, shards, row_count, width = source_rows.shape

    def flatten(array):
        return array.reshape((parts * shards,) + array.shape[2:])

    def unflatten(array):
        return array.reshape((parts, shards) + array.shape[1:])
    source, source_sums = (source_rows, source_state)
    target, target_sums = (target_rows, target_state)
    for bucket in range(STEPS):
        target = jnp.roll(target, 1, axis=0)
        target_sums = jnp.roll(target_sums, 1, axis=0)

        def per_device(packed):
            return train_bucket(*packed, relation_table)
        results = lax.map(per_device, (flatten(source), flatten(source_sums), flatten(target), flatten(target_sums), flatten(source_ids[:, :, bucket]), flatten(target_ids[:, :, bucket]), flatten(relation_ids[:, :, bucket]), flatten(negative_block[:, :, bucket]), flatten(edge_counts[:, :, bucket])))
        source, source_sums, target, target_sums = [unflatten(item) for item in results]
    published = source.astype(jnp.bfloat16)
    nothing = jnp.zeros((), jnp.bfloat16)
    pieces = []
    for shard in range(shards):
        keep = (serving_shard == shard) & (changed_rows == 1)
        pieces.append(jnp.where(keep[..., None], published, nothing))
    served = jnp.stack(pieces, axis=1)
    return (source, source_sums, target, target_sums, served)
```

```python
import functools
import jax
import jax.numpy as jnp
from jax import lax
from jax.experimental import pallas as pl
from jax.experimental.pallas import tpu as pltpu
from jax.sharding import PartitionSpec as P

LEARN_RATE = 0.1
EPSILON = 1e-08
BLOCK = 128
CHUNK = 256
MESH = pl.DeviceIdType.MESH
F32 = jnp.float32
BF16 = jnp.bfloat16


def dot(a, b, contract=((1,), (0,))):
    return lax.dot_general(a, b, (contract, ((), ())), preferred_element_type=F32)


def split(x):
    high = x.astype(BF16)
    return high, (x - high.astype(F32)).astype(BF16)


def down(row):
    return jnp.broadcast_to(row, (BLOCK, BLOCK)).T


def column(row):
    return jnp.broadcast_to(row, (8, row.shape[1])).T[:, :1]


def as_row(col):
    return jnp.broadcast_to(col, (col.shape[0], BLOCK)).T[:1, :]


def adagrad(weights, state_col, grad):
    state_col = state_col + jnp.mean(grad * grad, axis=-1, keepdims=True)
    rate = LEARN_RATE / (jnp.sqrt(state_col) + EPSILON)
    return weights - rate * grad, state_col


def kernel(
    dom, serve, steps, blocks,
    src, sst, tgt, tst, rel, sid, tid, rid, nb, cnt, shard, changed,
    o_src, o_sst, o_tgt, o_tst, o_served,
    ubuf, unew, mbuf, msend, code, code_in, pay, pay_in, expand,
    rstack, relg, qhi, qlo, whi, wlo,
    u_send, u_recv, m_send, m_recv, c_send, c_recv, p_send, p_recv,
):
    rows, width = src.shape
    nrel = rel.shape[0]
    chunks = blocks * BLOCK // CHUNK
    per = CHUNK // BLOCK
    slots = pay.shape[1]
    d = lax.axis_index("dom")
    s = lax.axis_index("serve")
    right, left = lax.rem(d + 1, dom), lax.rem(d + dom - 1, dom)
    peers = [lax.rem(s + j, serve) for j in range(1, serve)]

    barrier = pltpu.get_barrier_semaphore()
    for neighbour in (left, right):
        pl.semaphore_signal(barrier, inc=1, device_id=(neighbour, s), device_id_type=MESH)
    for peer in peers:
        pl.semaphore_signal(barrier, inc=1, device_id=(d, peer), device_id_type=MESH)
    msend[0] = jnp.broadcast_to(tst[...], (8, rows))
    code[...] = jnp.broadcast_to(
        jnp.where(changed[...] == 1, shard[...], -1).astype(F32), (8, rows)
    )
    pl.semaphore_wait(barrier, 2 + serve - 1)

    def ring(step, rows_ref):
        u = pltpu.make_async_remote_copy(
            src_ref=rows_ref, dst_ref=ubuf.at[step], send_sem=u_send.at[step],
            recv_sem=u_recv.at[step], device_id=(right, s), device_id_type=MESH)
        m = pltpu.make_async_remote_copy(
            src_ref=msend.at[step], dst_ref=mbuf.at[step], send_sem=m_send.at[step],
            recv_sem=m_recv.at[step], device_id=(right, s), device_id_type=MESH)
        u.start()
        m.start()
        return u, m

    moving = ring(0, tgt)
    code_copies = []
    for j, peer in enumerate(peers):
        c = pltpu.make_async_remote_copy(
            src_ref=code, dst_ref=code_in.at[j], send_sem=c_send.at[j],
            recv_sem=c_recv.at[j], device_id=(d, peer), device_id_type=MESH)
        c.start()
        code_copies.append(c)

    lane = lax.broadcasted_iota(jnp.int32, (CHUNK, BLOCK), 1).astype(F32)
    lane_rows = lax.broadcasted_iota(jnp.int32, (CHUNK, rows), 1)
    lane_rows_f = lane_rows.astype(F32)
    edge = lax.broadcasted_iota(jnp.int32, (CHUNK, 1), 0)
    sub_rows = lax.broadcasted_iota(jnp.int32, (rows, BLOCK), 0).astype(F32)

    def ids_down(ref, step, c):
        parts = [
            down(ref[step, c * per + i : c * per + i + 1, :].astype(F32)) for i in range(per)
        ]
        return jnp.concatenate(parts, axis=0)

    def one_hot(ids):
        wide = jnp.concatenate([ids] * (rows // BLOCK), axis=1)
        return wide == lane_rows_f

    def one_hot_t(ref, step, c):
        parts = [
            jnp.where(
                sub_rows == ref[step, c * per + i : c * per + i + 1, :].astype(F32), 1.0, 0.0
            ).astype(BF16)
            for i in range(per)
        ]
        return jnp.concatenate(parts, axis=1)

    rstack[...] = jnp.zeros_like(rstack)
    first, rest = rel[...], rel[...]
    for i in range(3):
        part = first.astype(BF16)
        rstack[i * nrel : (i + 1) * nrel, :] = part
        first = first - part.astype(F32)
    lane_i = lax.broadcasted_iota(jnp.int32, (CHUNK, BLOCK), 1)
    lane_rel = jnp.where(lane_i < 3 * nrel, lax.rem(lane_i, nrel), -1).astype(F32)

    def relations(step):
        for c in range(chunks):
            hot = jnp.where(ids_down(rid, step, c) == lane_rel, 1.0, 0.0).astype(BF16)
            at = (step * chunks + c) * CHUNK
            relg[at : at + CHUNK, :] = dot(hot, rstack[...])

    def queries(step, source):
        high, low = split(source)
        for c in range(chunks):
            hot = jnp.where(one_hot(ids_down(sid, step, c)), 1.0, 0.0).astype(BF16)
            rows_of = dot(hot, high) + dot(hot, low)
            at = (step * chunks + c) * CHUNK
            q_high, q_low = split(rows_of * relg[at : at + CHUNK, :])
            qhi[c * CHUNK : (c + 1) * CHUNK, :] = q_high
            qlo[c * CHUNK : (c + 1) * CHUNK, :] = q_low

    def weights(step, u_high, u_low):
        for c in range(chunks):
            at = slice(c * CHUNK, (c + 1) * CHUNK)
            a, b = qhi[at, :], qlo[at, :]
            nt = ((1,), (1,))
            logits = dot(a, u_high, nt) + dot(a, u_low, nt) + dot(b, u_high, nt)
            hot = one_hot(ids_down(tid, step, c))
            count = cnt[step, c * per]
            block = nb[step, c * per]
            for i in range(1, per):
                count = jnp.where(edge >= i * BLOCK, cnt[step, c * per + i] + i * BLOCK, count)
                block = jnp.where(edge >= i * BLOCK, nb[step, c * per + i], block)
            valid = jnp.where(edge < count, 1.0, 0.0)
            pos = jnp.sum(jnp.where(hot, logits, 0.0), axis=1, keepdims=True)
            dpos = -jax.nn.sigmoid(-pos) * valid
            negative = (lane_rows // BLOCK) == block
            dneg = jnp.where(negative, jax.nn.sigmoid(logits) * (valid / BLOCK), 0.0)
            w_high, w_low = split(jnp.where(hot, dpos, 0.0) + dneg)
            whi[at, :] = w_high
            wlo[at, :] = w_low

    def target_grad():
        total = jnp.zeros((rows, width), F32)
        for c in range(chunks):
            at = slice(c * CHUNK, (c + 1) * CHUNK)
            tn = ((0,), (0,))
            total += dot(whi[at, :], qhi[at, :], tn)
            total += dot(wlo[at, :], qhi[at, :], tn)
            total += dot(whi[at, :], qlo[at, :], tn)
        return total

    def source_grad(step, u_high, u_low):
        total = jnp.zeros((rows, width), F32)
        for c in range(chunks):
            at = slice(c * CHUNK, (c + 1) * CHUNK)
            g = dot(whi[at, :], u_high) + dot(wlo[at, :], u_high) + dot(whi[at, :], u_low)
            r = (step * chunks + c) * CHUNK
            g_high, g_low = split(g * relg[r : r + CHUNK, :])
            hot = one_hot_t(sid, step, c)
            total += dot(hot, g_high) + dot(hot, g_low)
        return total

    def compaction(code_row, which):
        sel = jnp.where(code_row == which.astype(F32), 1.0, 0.0)
        before = lax.broadcasted_iota(jnp.int32, (rows, rows), 0)
        after = lax.broadcasted_iota(jnp.int32, (rows, rows), 1)
        tri = jnp.where(before < after, 1.0, 0.0).astype(BF16)
        rank = dot(jnp.broadcast_to(sel, (16, rows)).astype(BF16), tri)[:1, :]
        slot = lax.broadcasted_iota(jnp.int32, (slots, rows), 0).astype(F32)
        return jnp.where((rank == slot) & (sel > 0.0), 1.0, 0.0)

    for step in range(steps):
        relations(step)
    source, source_state = src[...], column(sst[...])
    queries(0, source)
    for j in range(serve - 1):
        code_copies[j].wait()
        expand[j] = compaction(code_in[j, :1, :], s).T.astype(BF16)

    target = None
    for step in range(steps):
        last = step == steps - 1
        for copy in moving:
            copy.wait()
        target = ubuf[step]
        target_state = column(mbuf[step, :1, :])
        u_high, u_low = split(target)
        weights(step, u_high, u_low)
        if not last:
            target, target_state = adagrad(target, target_state, target_grad())
            unew[step] = target
            msend[step + 1] = jnp.broadcast_to(as_row(target_state), (8, rows))
            moving = ring(step + 1, unew.at[step])
            source, source_state = adagrad(
                source, source_state, source_grad(step, u_high, u_low))
            queries(step + 1, source)
        else:
            source, source_state = adagrad(
                source, source_state, source_grad(step, u_high, u_low))
            published = source.astype(BF16)
            pay_copies = []
            for j, peer in enumerate(peers):
                pick = compaction(code[:1, :], peer).astype(BF16)
                pay[j] = dot(pick, published).astype(BF16)
                p = pltpu.make_async_remote_copy(
                    src_ref=pay.at[j], dst_ref=pay_in.at[j], send_sem=p_send.at[j],
                    recv_sem=p_recv.at[j], device_id=(d, peer), device_id_type=MESH)
                p.start()
                pay_copies.append(p)
            target, target_state = adagrad(target, target_state, target_grad())
            o_tgt[...] = target
            o_tst[...] = as_row(target_state)
            o_src[...] = source
            o_sst[...] = as_row(source_state)
            own = column(code[:1, :]) == s.astype(F32)
            o_served[s] = jnp.where(own, source, 0.0).astype(BF16)
            for j in range(serve - 1):
                pay_copies[j].wait()
                sender = lax.rem(s + serve - 1 - j, serve)
                o_served[sender] = dot(expand[j], pay_in[j]).astype(BF16)


def on_device(
    dom, serve,
    source_rows, source_state, target_rows, target_state, relation_table,
    source_ids, target_ids, relation_ids, negative_block, edge_counts,
    serving_shard, changed_rows,
):
    _, _, rows, width = source_rows.shape
    _, _, steps, blocks, _ = source_ids.shape
    nrel = relation_table.shape[0]
    slots = rows // 4
    edges = blocks * BLOCK
    vmem = pl.BlockSpec(memory_space=pltpu.VMEM)
    smem = pl.BlockSpec(memory_space=pltpu.SMEM)
    dma = pltpu.SemaphoreType.DMA
    outs = pl.pallas_call(
        functools.partial(kernel, dom, serve, steps, blocks),
        out_shape=(
            jax.ShapeDtypeStruct((rows, width), F32),
            jax.ShapeDtypeStruct((1, rows), F32),
            jax.ShapeDtypeStruct((rows, width), F32),
            jax.ShapeDtypeStruct((1, rows), F32),
            jax.ShapeDtypeStruct((serve, rows, width), BF16),
        ),
        in_specs=[vmem] * 8 + [smem] * 2 + [vmem] * 2,
        out_specs=(vmem,) * 5,
        scratch_shapes=[
            pltpu.VMEM((steps, rows, width), F32),
            pltpu.VMEM((steps, rows, width), F32),
            pltpu.VMEM((steps, 8, rows), F32),
            pltpu.VMEM((steps, 8, rows), F32),
            pltpu.VMEM((8, rows), F32),
            pltpu.VMEM((serve - 1, 8, rows), F32),
            pltpu.VMEM((serve - 1, slots, width), BF16),
            pltpu.VMEM((serve - 1, slots, width), BF16),
            pltpu.VMEM((serve - 1, rows, slots), BF16),
            pltpu.VMEM((BLOCK, width), BF16),
            pltpu.VMEM((steps * edges, width), F32),
            pltpu.VMEM((edges, width), BF16),
            pltpu.VMEM((edges, width), BF16),
            pltpu.VMEM((edges, rows), BF16),
            pltpu.VMEM((edges, rows), BF16),
            dma((steps,)), dma((steps,)), dma((steps,)), dma((steps,)),
            dma((serve - 1,)), dma((serve - 1,)), dma((serve - 1,)), dma((serve - 1,)),
        ],
        compiler_params=pltpu.CompilerParams(
            collective_id=0, has_side_effects=True, vmem_limit_bytes=48 * 1024 * 1024
        ),
        name="train_and_publish",
    )(
        source_rows[0, 0], source_state[0], target_rows[0, 0], target_state[0],
        relation_table, source_ids[0, 0], target_ids[0, 0], relation_ids[0, 0],
        negative_block[0, 0], edge_counts[0, 0], serving_shard[0], changed_rows[0],
    )
    source, source_sums, target, target_sums, served = outs
    return (source[None, None], source_sums[None], target[None, None], target_sums[None],
            served[None, None])


def solution(mesh):
    rows4 = P("dom", "serve", None, None)
    rows3 = P("dom", "serve", None)
    ids = P("dom", "serve", None, None, None)
    return jax.shard_map(
        functools.partial(on_device, mesh.shape["dom"], mesh.shape["serve"]),
        mesh=mesh,
        in_specs=(rows4, rows3, rows4, rows3, P(), ids, ids, ids, rows4, rows4, rows3, rows3),
        out_specs=(rows4, rows3, rows4, rows3, ids),
        check_vma=False,
    )
```

```python
import functools
import jax
import jax.numpy as jnp
from jax import lax
from jax.experimental import pallas as pl
from jax.experimental.pallas import tpu as pltpu
from jax.sharding import PartitionSpec as P

LEARN_RATE = 0.1
EPSILON = 1e-08
BLOCK = 128
CHUNK = 256
WIRE_MAX = 32767.0
TINY = 1e-30
MESH = pl.DeviceIdType.MESH
F32 = jnp.float32
BF16 = jnp.bfloat16


def dot(a, b, contract=((1,), (0,))):
    return lax.dot_general(a, b, (contract, ((), ())), preferred_element_type=F32)


def split(x):
    high = x.astype(BF16)
    return high, (x - high.astype(F32)).astype(BF16)


def to_wire(u):
    most = jnp.maximum(jnp.max(jnp.abs(u), axis=0, keepdims=True), TINY)
    return jnp.floor(u * (WIRE_MAX / most) + 0.5).astype(jnp.int32).astype(jnp.int16), most


def from_wire(q, most):
    return q.astype(jnp.int32).astype(F32) * (most * (1.0 / WIRE_MAX))


def adagrad(weights, state, grad):
    state = state + jnp.mean(grad * grad, axis=0, keepdims=True)
    rate = LEARN_RATE / (jnp.sqrt(state) + EPSILON)
    return weights - rate * grad, state


def kernel(
    dom, serve, steps, blocks,
    src, sst, tgt, tst, rel, sid, tid, rid, nb, cnt, shard, changed,
    o_src, o_sst, o_tgt, o_tst, o_served,
    ubuf, wire, mbuf, msend, code, code_in, pay, pay_in, expand,
    relg, qhi, qlo, whi, wlo,
    u_send, u_recv, m_send, m_recv, c_send, c_recv, p_send, p_recv,
):
    width, rows = src.shape
    nrel = rel.shape[0]
    chunks = blocks * BLOCK // CHUNK
    per = CHUNK // BLOCK
    slots = pay.shape[1]
    nt = ((1,), (1,))
    d = lax.axis_index("dom")
    s = lax.axis_index("serve")
    right, left = lax.rem(d + 1, dom), lax.rem(d + dom - 1, dom)
    peers = [lax.rem(s + j, serve) for j in range(1, serve)]

    barrier = pltpu.get_barrier_semaphore()
    for neighbour in (left, right):
        pl.semaphore_signal(barrier, inc=1, device_id=(neighbour, s), device_id_type=MESH)
    for peer in peers:
        pl.semaphore_signal(barrier, inc=1, device_id=(d, peer), device_id_type=MESH)

    eight = lax.broadcasted_iota(jnp.int32, (8, rows), 0)
    wire[0], most = to_wire(tgt[...])
    msend[0] = jnp.where(eight == 0, tst[...], most)
    code[...] = jnp.broadcast_to(
        jnp.where(changed[...] == 1, shard[...], -1).astype(F32), (8, rows)
    )
    pl.semaphore_wait(barrier, 2 + serve - 1)

    def ring(step):
        u = pltpu.make_async_remote_copy(
            src_ref=wire.at[step], dst_ref=ubuf.at[step], send_sem=u_send.at[step],
            recv_sem=u_recv.at[step], device_id=(right, s), device_id_type=MESH)
        m = pltpu.make_async_remote_copy(
            src_ref=msend.at[step], dst_ref=mbuf.at[step], send_sem=m_send.at[step],
            recv_sem=m_recv.at[step], device_id=(right, s), device_id_type=MESH)
        u.start()
        m.start()
        return u, m

    moving = ring(0)
    code_copies = []
    for j, peer in enumerate(peers):
        c = pltpu.make_async_remote_copy(
            src_ref=code, dst_ref=code_in.at[j], send_sem=c_send.at[j],
            recv_sem=c_recv.at[j], device_id=(d, peer), device_id_type=MESH)
        c.start()
        code_copies.append(c)

    row_of = lax.broadcasted_iota(jnp.int32, (rows, CHUNK), 0)
    edge = lax.broadcasted_iota(jnp.int32, (1, CHUNK), 1)

    def ids(ref, step, c):
        return jnp.concatenate(
            [ref[step, c * per + i : c * per + i + 1, :] for i in range(per)], axis=1)

    def one_hot(ref, step, c):
        return row_of == ids(ref, step, c)

    def ones(mask):
        return jnp.where(mask, 1.0, 0.0).astype(BF16)

    def per_edge(ref, step, c, offset):
        value = ref[step, c * per]
        for i in range(1, per):
            value = jnp.where(edge >= i * BLOCK, ref[step, c * per + i] + i * offset, value)
        return value

    parts, rest = [], rel[...]
    for i in range(3):
        parts.append(rest.astype(BF16).astype(F32))
        rest = rest - parts[-1]
    parts.append(jnp.zeros((BLOCK - 3 * nrel, width), F32))
    table = jnp.concatenate(parts, axis=0).T.astype(BF16)
    sub = lax.broadcasted_iota(jnp.int32, (BLOCK, CHUNK), 0)
    rel_of = jnp.where(sub < 3 * nrel, lax.rem(sub, nrel), -1)

    def relations(step):
        for c in range(chunks):
            at = (step * chunks + c) * CHUNK
            relg[:, at : at + CHUNK] = dot(table, ones(rel_of == ids(rid, step, c)))

    def queries(step, source):
        high, low = split(source)
        for c in range(chunks):
            hot = ones(one_hot(sid, step, c))
            at = (step * chunks + c) * CHUNK
            q = (dot(high, hot) + dot(low, hot)) * relg[:, at : at + CHUNK]
            q_high, q_low = split(q)
            qhi[:, c * CHUNK : (c + 1) * CHUNK] = q_high
            qlo[:, c * CHUNK : (c + 1) * CHUNK] = q_low

    def weights(step, target):
        high, low = split(target.T)
        for c in range(chunks):
            at = slice(c * CHUNK, (c + 1) * CHUNK)
            a, b = qhi[:, at], qlo[:, at]
            logits = dot(high, a) + dot(low, a) + dot(high, b)
            hot = one_hot(tid, step, c)
            valid = jnp.where(edge < per_edge(cnt, step, c, BLOCK), 1.0, 0.0)
            pos = jnp.sum(jnp.where(hot, logits, 0.0), axis=0, keepdims=True)
            dpos = -jax.nn.sigmoid(-pos) * valid
            negative = (row_of // BLOCK) == per_edge(nb, step, c, 0)
            dneg = jnp.where(negative, jax.nn.sigmoid(logits) * (valid / BLOCK), 0.0)
            w_high, w_low = split(jnp.where(hot, dpos, 0.0) + dneg)
            whi[:, at] = w_high
            wlo[:, at] = w_low

    def target_grad():
        total = jnp.zeros((width, rows), F32)
        for c in range(chunks):
            at = slice(c * CHUNK, (c + 1) * CHUNK)
            total += dot(qhi[:, at], whi[:, at], nt)
            total += dot(qlo[:, at], whi[:, at], nt)
            total += dot(qhi[:, at], wlo[:, at], nt)
        return total

    def source_grad(step, target):
        high, low = split(target)
        total = jnp.zeros((width, rows), F32)
        for c in range(chunks):
            at = slice(c * CHUNK, (c + 1) * CHUNK)
            g = dot(high, whi[:, at]) + dot(low, whi[:, at]) + dot(high, wlo[:, at])
            r = (step * chunks + c) * CHUNK
            g_high, g_low = split(g * relg[:, r : r + CHUNK])
            hot = ones(one_hot(sid, step, c))
            total += dot(g_high, hot, nt) + dot(g_low, hot, nt)
        return total

    def compaction(code_row, which):
        sel = jnp.where(code_row == which.astype(F32), 1.0, 0.0)
        before = lax.broadcasted_iota(jnp.int32, (rows, rows), 0)
        after = lax.broadcasted_iota(jnp.int32, (rows, rows), 1)
        rank = dot(jnp.broadcast_to(sel, (16, rows)).astype(BF16), ones(before < after))[:1, :]
        slot = lax.broadcasted_iota(jnp.int32, (slots, rows), 0).astype(F32)
        return ones((rank == slot) & (sel > 0.0))

    for step in range(steps):
        relations(step)
    source, source_state = src[...], sst[...]
    queries(0, source)
    for j in range(serve - 1):
        code_copies[j].wait()
        expand[j] = compaction(code_in[j, :1, :], s)

    target = None
    for step in range(steps):
        last = step == steps - 1
        for copy in moving:
            copy.wait()
        target = from_wire(ubuf[step], mbuf[step, 1:2, :])
        target_state = mbuf[step, :1, :]
        old = target
        weights(step, old)
        if not last:
            target, target_state = adagrad(target, target_state, target_grad())
            wire[step + 1], most = to_wire(target)
            msend[step + 1] = jnp.where(eight == 0, target_state, most)
            moving = ring(step + 1)
            source, source_state = adagrad(source, source_state, source_grad(step, old))
            queries(step + 1, source)
        else:
            source, source_state = adagrad(source, source_state, source_grad(step, old))
            published = source.astype(BF16)
            pay_copies = []
            for j, peer in enumerate(peers):
                pay[j] = dot(compaction(code[:1, :], peer), published, nt).astype(BF16)
                p = pltpu.make_async_remote_copy(
                    src_ref=pay.at[j], dst_ref=pay_in.at[j], send_sem=p_send.at[j],
                    recv_sem=p_recv.at[j], device_id=(d, peer), device_id_type=MESH)
                p.start()
                pay_copies.append(p)
            target, target_state = adagrad(target, target_state, target_grad())
            o_tgt[...] = target
            o_tst[...] = target_state
            o_src[...] = source
            o_sst[...] = source_state
            own = code[:1, :] == s.astype(F32)
            o_served[s] = jnp.where(own, source, 0.0).astype(BF16)
            for j in range(serve - 1):
                pay_copies[j].wait()
                sender = lax.rem(s + serve - 1 - j, serve)
                o_served[sender] = dot(pay_in[j], expand[j], ((0,), (0,))).astype(BF16)


def on_device(
    dom, serve,
    source_rows, source_state, target_rows, target_state, relation_table,
    source_ids, target_ids, relation_ids, negative_block, edge_counts,
    serving_shard, changed_rows,
):
    _, _, rows, width = source_rows.shape
    _, _, steps, blocks, _ = source_ids.shape
    nrel = relation_table.shape[0]
    slots = rows // 4
    edges = blocks * BLOCK
    vmem = pl.BlockSpec(memory_space=pltpu.VMEM)
    smem = pl.BlockSpec(memory_space=pltpu.SMEM)
    dma = pltpu.SemaphoreType.DMA
    outs = pl.pallas_call(
        functools.partial(kernel, dom, serve, steps, blocks),
        out_shape=(
            jax.ShapeDtypeStruct((width, rows), F32),
            jax.ShapeDtypeStruct((1, rows), F32),
            jax.ShapeDtypeStruct((width, rows), F32),
            jax.ShapeDtypeStruct((1, rows), F32),
            jax.ShapeDtypeStruct((serve, width, rows), BF16),
        ),
        in_specs=[vmem] * 8 + [smem] * 2 + [vmem] * 2,
        out_specs=(vmem,) * 5,
        scratch_shapes=[
            pltpu.VMEM((steps, width, rows), jnp.int16),
            pltpu.VMEM((steps, width, rows), jnp.int16),
            pltpu.VMEM((steps, 8, rows), F32),
            pltpu.VMEM((steps, 8, rows), F32),
            pltpu.VMEM((8, rows), F32),
            pltpu.VMEM((serve - 1, 8, rows), F32),
            pltpu.VMEM((serve - 1, slots, width), BF16),
            pltpu.VMEM((serve - 1, slots, width), BF16),
            pltpu.VMEM((serve - 1, slots, rows), BF16),
            pltpu.VMEM((width, steps * edges), F32),
            pltpu.VMEM((width, edges), BF16),
            pltpu.VMEM((width, edges), BF16),
            pltpu.VMEM((rows, edges), BF16),
            pltpu.VMEM((rows, edges), BF16),
            dma((steps,)), dma((steps,)), dma((steps,)), dma((steps,)),
            dma((serve - 1,)), dma((serve - 1,)), dma((serve - 1,)), dma((serve - 1,)),
        ],
        compiler_params=pltpu.CompilerParams(
            collective_id=0, has_side_effects=True, vmem_limit_bytes=48 * 1024 * 1024
        ),
        name="train_and_publish",
    )(
        source_rows[0, 0].T, source_state[0], target_rows[0, 0].T, target_state[0],
        relation_table, source_ids[0, 0], target_ids[0, 0], relation_ids[0, 0],
        negative_block[0, 0], edge_counts[0, 0], serving_shard[0], changed_rows[0],
    )
    source, source_sums, target, target_sums, served = outs
    return (source.T[None, None], source_sums[None], target.T[None, None], target_sums[None],
            jnp.swapaxes(served, 1, 2)[None, None])


def solution(mesh):
    rows4 = P("dom", "serve", None, None)
    rows3 = P("dom", "serve", None)
    ids = P("dom", "serve", None, None, None)
    return jax.shard_map(
        functools.partial(on_device, mesh.shape["dom"], mesh.shape["serve"]),
        mesh=mesh,
        in_specs=(rows4, rows3, rows4, rows3, P(), ids, ids, ids, rows4, rows4, rows3, rows3),
        out_specs=(rows4, rows3, rows4, rows3, ids),
        check_vma=False,
    )
```

```python
import functools
import jax
import jax.numpy as jnp
from jax import lax
from jax.experimental import pallas as pl
from jax.experimental.pallas import tpu as pltpu
from jax.sharding import PartitionSpec as P

LEARN_RATE = 0.1
EPSILON = 1e-08
BLOCK = 128
CHUNK = 256
WIRE_MAX = 32767.0
TINY = 1e-30
MESH = pl.DeviceIdType.MESH
F32 = jnp.float32
BF16 = jnp.bfloat16


def dot(a, b, contract=((1,), (0,))):
    return lax.dot_general(a, b, (contract, ((), ())), preferred_element_type=F32)


def split(x):
    high = x.astype(BF16)
    return high, (x - high.astype(F32)).astype(BF16)


def to_wire(u):
    most = jnp.maximum(jnp.max(jnp.abs(u), axis=0, keepdims=True), TINY)
    return jnp.floor(u * (WIRE_MAX / most) + 0.5).astype(jnp.int32).astype(jnp.int16), most


def from_wire(q, most):
    return q.astype(jnp.int32).astype(F32) * (most * (1.0 / WIRE_MAX))


def adagrad(weights, state, grad):
    state = state + jnp.mean(grad * grad, axis=0, keepdims=True)
    rate = LEARN_RATE / (jnp.sqrt(state) + EPSILON)
    return weights - rate * grad, state


def kernel(
    dom, serve, steps, blocks,
    src_in, sst_in, tgt_in, tst_in, rel_in, sid_in, tid_in, rid_in, nb_in, cnt_in, shard_in,
    changed_in,
    o_src, o_sst, o_tgt, o_tst, o_pay, o_expand, o_code,
    new_src, new_sst, new_tgt, new_tst, expand, own,
    src, sst, tgt, tst, rel, sid, tid, rid, nb, cnt, shard, changed,
    ubuf, wire, mbuf, msend, code, code_in, pay, pay_in, pick,
    relg, qhi, qlo, whi, wlo,
    loaded, stored, u_send, u_recv, m_send, m_recv, c_send, c_recv, p_send, p_recv,
):
    width, rows = src.shape
    nrel = rel.shape[0]
    chunks = blocks * BLOCK // CHUNK
    per = CHUNK // BLOCK
    slots = pay.shape[1]
    nt = ((1,), (1,))
    d = lax.axis_index("dom")
    s = lax.axis_index("serve")
    right, left = lax.rem(d + 1, dom), lax.rem(d + dom - 1, dom)
    peers = [lax.rem(s + j, serve) for j in range(1, serve)]

    loads = {}
    for i, (name, given, held) in enumerate((
        ("tgt", tgt_in, tgt), ("tst", tst_in, tst), ("shard", shard_in, shard),
        ("changed", changed_in, changed), ("rel", rel_in, rel), ("rid", rid_in, rid),
        ("src", src_in, src), ("sid", sid_in, sid), ("sst", sst_in, sst), ("tid", tid_in, tid),
        ("nb", nb_in, nb), ("cnt", cnt_in, cnt),
    )):
        loads[name] = pltpu.make_async_copy(given, held, loaded.at[i])
        loads[name].start()

    def arrived(*names):
        for name in names:
            loads[name].wait()

    barrier = pltpu.get_barrier_semaphore()
    for neighbour in (left, right):
        pl.semaphore_signal(barrier, inc=1, device_id=(neighbour, s), device_id_type=MESH)
    for peer in peers:
        pl.semaphore_signal(barrier, inc=1, device_id=(d, peer), device_id_type=MESH)

    eight = lax.broadcasted_iota(jnp.int32, (8, rows), 0)
    arrived("tgt", "tst")
    wire[0], most = to_wire(tgt[...])
    msend[0] = jnp.where(eight == 0, tst[...], most)
    arrived("shard", "changed")
    code[...] = jnp.broadcast_to(
        jnp.where(changed[...] == 1, shard[...], -1).astype(F32), (8, rows)
    )
    pl.semaphore_wait(barrier, 2 + serve - 1)

    def ring(step):
        u = pltpu.make_async_remote_copy(
            src_ref=wire.at[step], dst_ref=ubuf.at[step], send_sem=u_send.at[step],
            recv_sem=u_recv.at[step], device_id=(right, s), device_id_type=MESH)
        m = pltpu.make_async_remote_copy(
            src_ref=msend.at[step], dst_ref=mbuf.at[step], send_sem=m_send.at[step],
            recv_sem=m_recv.at[step], device_id=(right, s), device_id_type=MESH)
        u.start()
        m.start()
        return u, m

    moving = ring(0)
    code_copies = []
    for j, peer in enumerate(peers):
        c = pltpu.make_async_remote_copy(
            src_ref=code, dst_ref=code_in.at[j], send_sem=c_send.at[j],
            recv_sem=c_recv.at[j], device_id=(d, peer), device_id_type=MESH)
        c.start()
        code_copies.append(c)

    row_of = lax.broadcasted_iota(jnp.int32, (rows, CHUNK), 0)
    edge = lax.broadcasted_iota(jnp.int32, (1, CHUNK), 1)

    def ids(ref, step, c):
        return jnp.concatenate(
            [ref[step, c * per + i : c * per + i + 1, :] for i in range(per)], axis=1)

    def one_hot(ref, step, c):
        return row_of == ids(ref, step, c)

    def ones(mask):
        return jnp.where(mask, 1.0, 0.0).astype(BF16)

    def per_edge(ref, step, c, offset):
        return jnp.concatenate([
            jnp.broadcast_to(ref[step : step + 1, c * per + i : c * per + i + 1], (1, BLOCK))
            + i * offset
            for i in range(per)
        ], axis=1)

    arrived("rel", "rid")
    parts, rest = [], rel[...]
    for i in range(3):
        parts.append(rest.astype(BF16).astype(F32))
        rest = rest - parts[-1]
    parts.append(jnp.zeros((BLOCK - 3 * nrel, width), F32))
    table = jnp.concatenate(parts, axis=0).T.astype(BF16)
    sub = lax.broadcasted_iota(jnp.int32, (BLOCK, CHUNK), 0)
    rel_of = jnp.where(sub < 3 * nrel, lax.rem(sub, nrel), -1)

    def relations(step):
        for c in range(chunks):
            at = (step * chunks + c) * CHUNK
            relg[:, at : at + CHUNK] = dot(table, ones(rel_of == ids(rid, step, c)))

    def queries(step, source):
        high, low = split(source)
        for c in range(chunks):
            hot = ones(one_hot(sid, step, c))
            at = (step * chunks + c) * CHUNK
            q = (dot(high, hot) + dot(low, hot)) * relg[:, at : at + CHUNK]
            q_high, q_low = split(q)
            qhi[:, c * CHUNK : (c + 1) * CHUNK] = q_high
            qlo[:, c * CHUNK : (c + 1) * CHUNK] = q_low

    def weights(step, target):
        high, low = split(target.T)
        for c in range(chunks):
            at = slice(c * CHUNK, (c + 1) * CHUNK)
            a, b = qhi[:, at], qlo[:, at]
            logits = dot(high, a) + dot(low, a) + dot(high, b)
            hot = one_hot(tid, step, c)
            valid = jnp.where(edge < per_edge(cnt, step, c, BLOCK), 1.0, 0.0)
            pos = jnp.sum(jnp.where(hot, logits, 0.0), axis=0, keepdims=True)
            dpos = -jax.nn.sigmoid(-pos) * valid
            negative = (row_of // BLOCK) == per_edge(nb, step, c, 0)
            dneg = jnp.where(negative, jax.nn.sigmoid(logits) * (valid / BLOCK), 0.0)
            w_high, w_low = split(jnp.where(hot, dpos, 0.0) + dneg)
            whi[:, at] = w_high
            wlo[:, at] = w_low

    def target_grad():
        total = jnp.zeros((width, rows), F32)
        for c in range(chunks):
            at = slice(c * CHUNK, (c + 1) * CHUNK)
            total += dot(qhi[:, at], whi[:, at], nt)
            total += dot(qlo[:, at], whi[:, at], nt)
            total += dot(qhi[:, at], wlo[:, at], nt)
        return total

    def source_grad(step, target):
        high, low = split(target)
        total = jnp.zeros((width, rows), F32)
        for c in range(chunks):
            at = slice(c * CHUNK, (c + 1) * CHUNK)
            g = dot(high, whi[:, at]) + dot(low, whi[:, at]) + dot(high, wlo[:, at])
            r = (step * chunks + c) * CHUNK
            g_high, g_low = split(g * relg[:, r : r + CHUNK])
            hot = ones(one_hot(sid, step, c))
            total += dot(g_high, hot, nt) + dot(g_low, hot, nt)
        return total

    def compaction(code_row, which):
        sel = jnp.where(code_row == which.astype(F32), 1.0, 0.0)
        before = lax.broadcasted_iota(jnp.int32, (rows, rows), 0)
        after = lax.broadcasted_iota(jnp.int32, (rows, rows), 1)
        rank = dot(jnp.broadcast_to(sel, (16, rows)).astype(BF16), ones(before < after))[:1, :]
        slot = lax.broadcasted_iota(jnp.int32, (slots, rows), 0).astype(F32)
        return ones((rank == slot) & (sel > 0.0))

    for step in range(steps):
        relations(step)
    arrived("src", "sid")
    source = src[...]
    queries(0, source)
    arrived("sst", "tid", "nb", "cnt")
    source_state = sst[...]
    own[...] = jnp.where(code[:1, :] == s.astype(F32), 1.0, 0.0)
    for j, peer in enumerate(peers):
        pick[j] = compaction(code[:1, :], peer)
    for j in range(serve - 1):
        code_copies[j].wait()
        expand[j] = compaction(code_in[j, :1, :], s)

    stores = []

    def store(*pairs):
        for held, out in pairs:
            copy = pltpu.make_async_copy(held, out, stored.at[len(stores)])
            copy.start()
            stores.append(copy)

    store((expand, o_expand), (own, o_code))
    target = None
    for step in range(steps):
        last = step == steps - 1
        for copy in moving:
            copy.wait()
        target = from_wire(ubuf[step], mbuf[step, 1:2, :])
        target_state = mbuf[step, :1, :]
        old = target
        weights(step, old)
        if not last:
            target, target_state = adagrad(target, target_state, target_grad())
            wire[step + 1], most = to_wire(target)
            msend[step + 1] = jnp.where(eight == 0, target_state, most)
            moving = ring(step + 1)
            source, source_state = adagrad(source, source_state, source_grad(step, old))
            queries(step + 1, source)
        else:
            source, source_state = adagrad(source, source_state, source_grad(step, old))
            published = source.astype(BF16)
            pay_copies = []
            for j, peer in enumerate(peers):
                pay[j] = dot(pick[j], published, nt).astype(BF16)
                p = pltpu.make_async_remote_copy(
                    src_ref=pay.at[j], dst_ref=pay_in.at[j], send_sem=p_send.at[j],
                    recv_sem=p_recv.at[j], device_id=(d, peer), device_id_type=MESH)
                p.start()
                pay_copies.append(p)
            new_src[...] = source
            new_sst[...] = source_state
            store((new_src, o_src), (new_sst, o_sst))
            target, target_state = adagrad(target, target_state, target_grad())
            new_tgt[...] = target
            new_tst[...] = target_state
            store((new_tgt, o_tgt), (new_tst, o_tst))
            for j in range(serve - 1):
                pay_copies[j].wait()
            store((pay_in, o_pay))
            for copy in stores:
                copy.wait()


def finish(serve, src, sst, tgt, tst, pay_in, expand_in, own_in, *refs):
    (o_src, o_sst, o_tgt, o_tst, o_served,
     served, source, pay, expand, own, loaded, stored, served_sems) = refs
    loads = [
        pltpu.make_async_copy(given, held, loaded.at[i])
        for i, (given, held) in enumerate(
            ((pay_in, pay), (expand_in, expand), (src, source), (own_in, own)))
    ]
    copies = [
        pltpu.make_async_copy(given, out, stored.at[i])
        for i, (given, out) in enumerate(
            ((src, o_src), (tgt, o_tgt), (sst, o_sst), (tst, o_tst)))
    ]
    for copy in loads + copies:
        copy.start()
    s = lax.axis_index("serve")
    for load in loads[:2]:
        load.wait()
    for j in range(1, serve + 1):
        if j == serve:
            for load in loads[2:]:
                load.wait()
            piece = jnp.where(own[...] > 0.0, source[...], 0.0)
        else:
            piece = dot(pay[j - 1], expand[j - 1], ((0,), (0,)))
        served[j - 1] = piece.astype(BF16)
        sender = lax.rem(s + serve - j, serve)
        copy = pltpu.make_async_copy(served.at[j - 1], o_served.at[sender], served_sems.at[j - 1])
        copy.start()
        copies.append(copy)
    for copy in copies:
        copy.wait()


def on_device(
    dom, serve,
    source_rows, source_state, target_rows, target_state, relation_table,
    source_ids, target_ids, relation_ids, negative_block, edge_counts,
    serving_shard, changed_rows,
):
    _, _, rows, width = source_rows.shape
    _, _, steps, blocks, _ = source_ids.shape
    nrel = relation_table.shape[0]
    slots = rows // 4
    edges = blocks * BLOCK
    hbm = pl.BlockSpec(memory_space=pltpu.HBM)
    dma = pltpu.SemaphoreType.DMA
    args = (
        source_rows[0, 0].T, source_state[0], target_rows[0, 0].T, target_state[0],
        relation_table, source_ids[0, 0], target_ids[0, 0], relation_ids[0, 0],
        negative_block[0, 0], edge_counts[0, 0], serving_shard[0], changed_rows[0],
    )
    state = (
        jax.ShapeDtypeStruct((width, rows), F32),
        jax.ShapeDtypeStruct((1, rows), F32),
        jax.ShapeDtypeStruct((width, rows), F32),
        jax.ShapeDtypeStruct((1, rows), F32),
    )
    handed = state + (
        jax.ShapeDtypeStruct((serve - 1, slots, width), BF16),
        jax.ShapeDtypeStruct((serve - 1, slots, rows), BF16),
        jax.ShapeDtypeStruct((1, rows), F32),
    )
    outs = pl.pallas_call(
        functools.partial(kernel, dom, serve, steps, blocks),
        out_shape=handed,
        in_specs=[hbm] * len(args),
        out_specs=(hbm,) * len(handed),
        scratch_shapes=[
            pltpu.VMEM(held.shape, held.dtype) for held in state + handed[5:] + args
        ] + [
            pltpu.VMEM((steps, width, rows), jnp.int16),
            pltpu.VMEM((steps, width, rows), jnp.int16),
            pltpu.VMEM((steps, 8, rows), F32),
            pltpu.VMEM((steps, 8, rows), F32),
            pltpu.VMEM((8, rows), F32),
            pltpu.VMEM((serve - 1, 8, rows), F32),
            pltpu.VMEM((serve - 1, slots, width), BF16),
            pltpu.VMEM((serve - 1, slots, width), BF16),
            pltpu.VMEM((serve - 1, slots, rows), BF16),
            pltpu.VMEM((width, steps * edges), F32),
            pltpu.VMEM((width, edges), BF16),
            pltpu.VMEM((width, edges), BF16),
            pltpu.VMEM((rows, edges), BF16),
            pltpu.VMEM((rows, edges), BF16),
            dma((len(args),)), dma((len(handed),)),
            dma((steps,)), dma((steps,)), dma((steps,)), dma((steps,)),
            dma((serve - 1,)), dma((serve - 1,)), dma((serve - 1,)), dma((serve - 1,)),
        ],
        compiler_params=pltpu.CompilerParams(
            collective_id=0, has_side_effects=True, vmem_limit_bytes=60 * 1024 * 1024
        ),
        name="train",
    )(*args)
    source, source_sums, target, target_sums, served = pl.pallas_call(
        functools.partial(finish, serve),
        out_shape=state + (jax.ShapeDtypeStruct((serve, width, rows), BF16),),
        in_specs=[hbm] * len(handed),
        out_specs=(hbm,) * 5,
        scratch_shapes=[
            pltpu.VMEM((serve, width, rows), BF16),
            pltpu.VMEM((width, rows), F32),
            pltpu.VMEM(handed[4].shape, BF16),
            pltpu.VMEM(handed[5].shape, BF16),
            pltpu.VMEM((1, rows), F32),
            dma((4,)), dma((4,)), dma((serve,)),
        ],
        compiler_params=pltpu.CompilerParams(vmem_limit_bytes=60 * 1024 * 1024),
        name="publish",
    )(*outs)
    return (source.T[None, None], source_sums[None], target.T[None, None], target_sums[None],
            jnp.swapaxes(served, 1, 2)[None, None])


def solution(mesh):
    rows4 = P("dom", "serve", None, None)
    rows3 = P("dom", "serve", None)
    ids = P("dom", "serve", None, None, None)
    return jax.shard_map(
        functools.partial(on_device, mesh.shape["dom"], mesh.shape["serve"]),
        mesh=mesh,
        in_specs=(rows4, rows3, rows4, rows3, P(), ids, ids, ids, rows4, rows4, rows3, rows3),
        out_specs=(rows4, rows3, rows4, rows3, ids),
        check_vma=False,
    )
```

```python
import functools
import jax
import jax.numpy as jnp
from jax import lax
from jax.experimental import pallas as pl
from jax.experimental.pallas import tpu as pltpu
from jax.sharding import PartitionSpec as P

LEARN_RATE = 0.1
EPSILON = 1e-08
BLOCK = 128
CHUNK = 256
WIRE_MAX = 32767.0
TINY = 1e-30
MESH = pl.DeviceIdType.MESH
F32 = jnp.float32
BF16 = jnp.bfloat16


def dot(a, b, contract=((1,), (0,))):
    return lax.dot_general(a, b, (contract, ((), ())), preferred_element_type=F32)


def split(x):
    high = x.astype(BF16)
    return high, (x - high.astype(F32)).astype(BF16)


def to_wire(u):
    most = jnp.maximum(jnp.max(jnp.abs(u), axis=0, keepdims=True), TINY)
    return jnp.floor(u * (WIRE_MAX / most) + 0.5).astype(jnp.int32).astype(jnp.int16), most


def from_wire(q, most):
    return q.astype(jnp.int32).astype(F32) * (most * (1.0 / WIRE_MAX))


def adagrad(weights, state, grad):
    state = state + jnp.mean(grad * grad, axis=0, keepdims=True)
    rate = LEARN_RATE / (jnp.sqrt(state) + EPSILON)
    return weights - rate * grad, state


def kernel(
    dom, serve, steps, blocks,
    src_in, sst_in, tgt_in, tst_in, rel_in, sid_in, tid_in, rid_in, nb_in, cnt_in, shard_in,
    changed_in,
    o_src, o_sst, o_tgt, o_tst, o_pay, o_expand, o_code,
    new_src, new_sst, new_tgt, new_tst, expand, own,
    src, sst, tgt, tst, rel, sid, tid, rid, nb, cnt, shard, changed,
    ubuf, wire, mbuf, msend, code, code_in, pay, pay_in, pick,
    relg, qhi, qlo, whi, wlo,
    loaded, stored, u_send, u_recv, m_send, m_recv, c_send, c_recv, p_send, p_recv,
):
    width, rows = src.shape
    nrel = rel.shape[0]
    chunks = blocks * BLOCK // CHUNK
    per = CHUNK // BLOCK
    slots = pay.shape[1]
    nt = ((1,), (1,))
    d = lax.axis_index("dom")
    s = lax.axis_index("serve")
    right, left = lax.rem(d + 1, dom), lax.rem(d + dom - 1, dom)
    peers = [lax.rem(s + j, serve) for j in range(1, serve)]

    loads = {}
    for i, (name, given, held) in enumerate((
        ("tgt", tgt_in, tgt), ("tst", tst_in, tst), ("shard", shard_in, shard),
        ("changed", changed_in, changed), ("rel", rel_in, rel), ("rid", rid_in, rid),
        ("src", src_in, src), ("sid", sid_in, sid), ("sst", sst_in, sst), ("tid", tid_in, tid),
        ("nb", nb_in, nb), ("cnt", cnt_in, cnt),
    )):
        loads[name] = pltpu.make_async_copy(given, held, loaded.at[i])
        loads[name].start()

    def arrived(*names):
        for name in names:
            loads[name].wait()

    barrier = pltpu.get_barrier_semaphore()
    for neighbour in (left, right):
        pl.semaphore_signal(barrier, inc=1, device_id=(neighbour, s), device_id_type=MESH)
    for peer in peers:
        pl.semaphore_signal(barrier, inc=1, device_id=(d, peer), device_id_type=MESH)

    eight = lax.broadcasted_iota(jnp.int32, (8, rows), 0)
    arrived("tgt", "tst")
    wire[0], most = to_wire(tgt[...])
    msend[0] = jnp.where(eight == 0, tst[...], most)
    arrived("shard", "changed")
    code[...] = jnp.broadcast_to(
        jnp.where(changed[...] == 1, shard[...], -1).astype(F32), (8, rows)
    )
    pl.semaphore_wait(barrier, 2 + serve - 1)

    def ring(step):
        u = pltpu.make_async_remote_copy(
            src_ref=wire.at[step], dst_ref=ubuf.at[step], send_sem=u_send.at[step],
            recv_sem=u_recv.at[step], device_id=(right, s), device_id_type=MESH)
        m = pltpu.make_async_remote_copy(
            src_ref=msend.at[step], dst_ref=mbuf.at[step], send_sem=m_send.at[step],
            recv_sem=m_recv.at[step], device_id=(right, s), device_id_type=MESH)
        u.start()
        m.start()
        return u, m

    moving = ring(0)
    code_copies = []
    for j, peer in enumerate(peers):
        c = pltpu.make_async_remote_copy(
            src_ref=code, dst_ref=code_in.at[j], send_sem=c_send.at[j],
            recv_sem=c_recv.at[j], device_id=(d, peer), device_id_type=MESH)
        c.start()
        code_copies.append(c)

    row_of = lax.broadcasted_iota(jnp.int32, (rows, CHUNK), 0)
    edge = lax.broadcasted_iota(jnp.int32, (1, CHUNK), 1)

    def ids(ref, step, c):
        return jnp.concatenate(
            [ref[step, c * per + i : c * per + i + 1, :] for i in range(per)], axis=1)

    def one_hot(ref, step, c):
        return row_of == ids(ref, step, c)

    def ones(mask):
        return jnp.where(mask, 1.0, 0.0).astype(BF16)

    def per_edge(ref, step, c, offset):
        return jnp.concatenate([
            jnp.broadcast_to(ref[step : step + 1, c * per + i : c * per + i + 1], (1, BLOCK))
            + i * offset
            for i in range(per)
        ], axis=1)

    arrived("rel", "rid")
    parts, rest = [], rel[...]
    for i in range(3):
        parts.append(rest.astype(BF16).astype(F32))
        rest = rest - parts[-1]
    parts.append(jnp.zeros((BLOCK - 3 * nrel, width), F32))
    table = jnp.concatenate(parts, axis=0).T.astype(BF16)
    sub = lax.broadcasted_iota(jnp.int32, (BLOCK, CHUNK), 0)
    rel_of = jnp.where(sub < 3 * nrel, lax.rem(sub, nrel), -1)

    def relations(step):
        for c in range(chunks):
            at = (step * chunks + c) * CHUNK
            relg[:, at : at + CHUNK] = dot(table, ones(rel_of == ids(rid, step, c)))

    def queries(step, source):
        high, low = split(source)
        for c in range(chunks):
            hot = ones(one_hot(sid, step, c))
            at = (step * chunks + c) * CHUNK
            q = (dot(high, hot) + dot(low, hot)) * relg[:, at : at + CHUNK]
            q_high, q_low = split(q)
            qhi[:, c * CHUNK : (c + 1) * CHUNK] = q_high
            qlo[:, c * CHUNK : (c + 1) * CHUNK] = q_low

    def weights(step, target):
        high, low = split(target.T)
        for c in range(chunks):
            at = slice(c * CHUNK, (c + 1) * CHUNK)
            a, b = qhi[:, at], qlo[:, at]
            logits = dot(high, a) + dot(low, a) + dot(high, b)
            hot = one_hot(tid, step, c)
            valid = jnp.where(edge < per_edge(cnt, step, c, BLOCK), 1.0, 0.0)
            pos = jnp.sum(jnp.where(hot, logits, 0.0), axis=0, keepdims=True)
            dpos = -jax.nn.sigmoid(-pos) * valid
            negative = (row_of // BLOCK) == per_edge(nb, step, c, 0)
            dneg = jnp.where(negative, jax.nn.sigmoid(logits) * (valid / BLOCK), 0.0)
            w_high, w_low = split(jnp.where(hot, dpos, 0.0) + dneg)
            whi[:, at] = w_high
            wlo[:, at] = w_low

    def target_grad():
        total = jnp.zeros((width, rows), F32)
        for c in range(chunks):
            at = slice(c * CHUNK, (c + 1) * CHUNK)
            total += dot(qhi[:, at], whi[:, at], nt)
            total += dot(qlo[:, at], whi[:, at], nt)
            total += dot(qhi[:, at], wlo[:, at], nt)
        return total

    def source_grad(step, target):
        high, low = split(target)
        total = jnp.zeros((width, rows), F32)
        for c in range(chunks):
            at = slice(c * CHUNK, (c + 1) * CHUNK)
            g = dot(high, whi[:, at]) + dot(low, whi[:, at]) + dot(high, wlo[:, at])
            r = (step * chunks + c) * CHUNK
            g_high, g_low = split(g * relg[:, r : r + CHUNK])
            hot = ones(one_hot(sid, step, c))
            total += dot(g_high, hot, nt) + dot(g_low, hot, nt)
        return total

    def compaction(code_row, which):
        sel = jnp.where(code_row == which.astype(F32), 1.0, 0.0)
        before = lax.broadcasted_iota(jnp.int32, (rows, rows), 0)
        after = lax.broadcasted_iota(jnp.int32, (rows, rows), 1)
        rank = dot(jnp.broadcast_to(sel, (16, rows)).astype(BF16), ones(before < after))[:1, :]
        slot = lax.broadcasted_iota(jnp.int32, (slots, rows), 0).astype(F32)
        return ones((rank == slot) & (sel > 0.0))

    for step in range(steps):
        relations(step)
    arrived("src", "sid")
    source = src[...]
    queries(0, source)
    arrived("sst", "tid", "nb", "cnt")
    source_state = sst[...]
    own[...] = jnp.where(code[:1, :] == s.astype(F32), 1.0, 0.0)
    for j, peer in enumerate(peers):
        pick[j] = compaction(code[:1, :], peer)
    for j in range(serve - 1):
        code_copies[j].wait()
        expand[j] = compaction(code_in[j, :1, :], s)

    stores = []

    def store(*pairs):
        for held, out in pairs:
            copy = pltpu.make_async_copy(held, out, stored.at[len(stores)])
            copy.start()
            stores.append(copy)

    store((expand, o_expand), (own, o_code))
    target = None
    for step in range(steps):
        last = step == steps - 1
        for copy in moving:
            copy.wait()
        target = from_wire(ubuf[step], mbuf[step, 1:2, :])
        target_state = mbuf[step, :1, :]
        old = target
        weights(step, old)
        if not last:
            target, target_state = adagrad(target, target_state, target_grad())
            wire[step + 1], most = to_wire(target)
            msend[step + 1] = jnp.where(eight == 0, target_state, most)
            moving = ring(step + 1)
            source, source_state = adagrad(source, source_state, source_grad(step, old))
            queries(step + 1, source)
        else:
            source, source_state = adagrad(source, source_state, source_grad(step, old))
            published = source.astype(BF16)
            pay_copies = []
            for j, peer in enumerate(peers):
                pay[j] = dot(pick[j], published, nt).astype(BF16)
                p = pltpu.make_async_remote_copy(
                    src_ref=pay.at[j], dst_ref=pay_in.at[j], send_sem=p_send.at[j],
                    recv_sem=p_recv.at[j], device_id=(d, peer), device_id_type=MESH)
                p.start()
                pay_copies.append(p)
            new_src[...] = source
            new_sst[...] = source_state
            store((new_src, o_src), (new_sst, o_sst))
            target, target_state = adagrad(target, target_state, target_grad())
            new_tgt[...] = target
            new_tst[...] = target_state
            store((new_tgt, o_tgt), (new_tst, o_tst))
            for j in range(serve - 1):
                pay_copies[j].wait()
            store((pay_in, o_pay))
            for copy in stores:
                copy.wait()


def finish(serve, *refs):
    given, outs, held = refs[:7], refs[7:11], refs[12:19]
    o_served, served, loaded, stored, served_sems = refs[11], *refs[19:]
    src, _, _, _, pay, expand, own = held
    order = (4, 5, 0, 6, 2, 1, 3)
    loads = {i: pltpu.make_async_copy(given[i], held[i], loaded.at[i]) for i in order}
    for i in order:
        loads[i].start()
    copies = []

    def store(value, out, sem):
        copies.append(pltpu.make_async_copy(value, out, sem))
        copies[-1].start()

    s = lax.axis_index("serve")
    loads[4].wait()
    loads[5].wait()
    for j in range(1, serve + 1):
        if j == serve:
            for i in order[2:]:
                loads[i].wait()
                if i < 4:
                    store(held[i], outs[i], stored.at[i])
            piece = jnp.where(own[...] > 0.0, src[...], 0.0)
        else:
            piece = dot(pay[j - 1], expand[j - 1], ((0,), (0,)))
        served[j - 1] = piece.astype(BF16)
        sender = lax.rem(s + serve - j, serve)
        store(served.at[j - 1], o_served.at[sender], served_sems.at[j - 1])
    for copy in copies:
        copy.wait()


def on_device(
    dom, serve,
    source_rows, source_state, target_rows, target_state, relation_table,
    source_ids, target_ids, relation_ids, negative_block, edge_counts,
    serving_shard, changed_rows,
):
    _, _, rows, width = source_rows.shape
    _, _, steps, blocks, _ = source_ids.shape
    nrel = relation_table.shape[0]
    slots = rows // 4
    edges = blocks * BLOCK
    hbm = pl.BlockSpec(memory_space=pltpu.HBM)
    dma = pltpu.SemaphoreType.DMA
    args = (
        source_rows[0, 0].T, source_state[0], target_rows[0, 0].T, target_state[0],
        relation_table, source_ids[0, 0], target_ids[0, 0], relation_ids[0, 0],
        negative_block[0, 0], edge_counts[0, 0], serving_shard[0], changed_rows[0],
    )
    state = (
        jax.ShapeDtypeStruct((width, rows), F32),
        jax.ShapeDtypeStruct((1, rows), F32),
        jax.ShapeDtypeStruct((width, rows), F32),
        jax.ShapeDtypeStruct((1, rows), F32),
    )
    handed = state + (
        jax.ShapeDtypeStruct((serve - 1, slots, width), BF16),
        jax.ShapeDtypeStruct((serve - 1, slots, rows), BF16),
        jax.ShapeDtypeStruct((1, rows), F32),
    )
    outs = pl.pallas_call(
        functools.partial(kernel, dom, serve, steps, blocks),
        out_shape=handed,
        in_specs=[hbm] * len(args),
        out_specs=(hbm,) * len(handed),
        scratch_shapes=[
            pltpu.VMEM(held.shape, held.dtype) for held in state + handed[5:] + args
        ] + [
            pltpu.VMEM((steps, width, rows), jnp.int16),
            pltpu.VMEM((steps, width, rows), jnp.int16),
            pltpu.VMEM((steps, 8, rows), F32),
            pltpu.VMEM((steps, 8, rows), F32),
            pltpu.VMEM((8, rows), F32),
            pltpu.VMEM((serve - 1, 8, rows), F32),
            pltpu.VMEM((serve - 1, slots, width), BF16),
            pltpu.VMEM((serve - 1, slots, width), BF16),
            pltpu.VMEM((serve - 1, slots, rows), BF16),
            pltpu.VMEM((width, steps * edges), F32),
            pltpu.VMEM((width, edges), BF16),
            pltpu.VMEM((width, edges), BF16),
            pltpu.VMEM((rows, edges), BF16),
            pltpu.VMEM((rows, edges), BF16),
            dma((len(args),)), dma((len(handed),)),
            dma((steps,)), dma((steps,)), dma((steps,)), dma((steps,)),
            dma((serve - 1,)), dma((serve - 1,)), dma((serve - 1,)), dma((serve - 1,)),
        ],
        compiler_params=pltpu.CompilerParams(
            collective_id=0, has_side_effects=True, vmem_limit_bytes=60 * 1024 * 1024
        ),
        name="train",
    )(*args)
    source, source_sums, target, target_sums, served = pl.pallas_call(
        functools.partial(finish, serve),
        out_shape=state + (jax.ShapeDtypeStruct((serve, width, rows), BF16),),
        in_specs=[hbm] * len(handed),
        out_specs=(hbm,) * 5,
        scratch_shapes=[pltpu.VMEM(held.shape, held.dtype) for held in handed] + [
            pltpu.VMEM((serve, width, rows), BF16),
            dma((len(handed),)), dma((4,)), dma((serve,)),
        ],
        compiler_params=pltpu.CompilerParams(vmem_limit_bytes=60 * 1024 * 1024),
        name="publish",
    )(*outs)
    return (source.T[None, None], source_sums[None], target.T[None, None], target_sums[None],
            jnp.swapaxes(served, 1, 2)[None, None])


def solution(mesh):
    rows4 = P("dom", "serve", None, None)
    rows3 = P("dom", "serve", None)
    ids = P("dom", "serve", None, None, None)
    return jax.shard_map(
        functools.partial(on_device, mesh.shape["dom"], mesh.shape["serve"]),
        mesh=mesh,
        in_specs=(rows4, rows3, rows4, rows3, P(), ids, ids, ids, rows4, rows4, rows3, rows3),
        out_specs=(rows4, rows3, rows4, rows3, ids),
        check_vma=False,
    )
```

```python
import functools
import jax
import jax.numpy as jnp
from jax import lax
from jax.experimental import pallas as pl
from jax.experimental.pallas import tpu as pltpu
from jax.sharding import PartitionSpec as P

LEARN_RATE = 0.1
EPSILON = 1e-08
BLOCK = 128
CHUNK = 256
WIRE_MAX = 32767.0
TINY = 1e-30
MESH = pl.DeviceIdType.MESH
F32 = jnp.float32
BF16 = jnp.bfloat16


def dot(a, b, contract=((1,), (0,))):
    return lax.dot_general(a, b, (contract, ((), ())), preferred_element_type=F32)


def split(x):
    high = x.astype(BF16)
    return high, (x - high.astype(F32)).astype(BF16)


def to_wire(u):
    most = jnp.maximum(jnp.max(jnp.abs(u), axis=0, keepdims=True), TINY)
    return jnp.floor(u * (WIRE_MAX / most) + 0.5).astype(jnp.int32).astype(jnp.int16), most


def from_wire(q, most):
    return q.astype(jnp.int32).astype(F32) * (most * (1.0 / WIRE_MAX))


def adagrad(weights, state, grad):
    state = state + jnp.mean(grad * grad, axis=0, keepdims=True)
    rate = LEARN_RATE / (jnp.sqrt(state) + EPSILON)
    return weights - rate * grad, state


def kernel(
    dom, serve, steps, blocks,
    src_in, sst_in, tgt_in, tst_in, rel_in, sid_in, tid_in, rid_in, nb_in, cnt_in, shard_in,
    changed_in,
    o_src, o_sst, o_tgt, o_tst, o_pay, o_expand, o_code,
    new_src, new_sst, new_tgt, new_tst, expand, own,
    src, sst, tgt, tst, rel, sid, tid, rid, nb, cnt, shard, changed,
    ubuf, wire, mbuf, msend, code, code_in, pay, pay_in, pick,
    relg, qhi, qlo, whi, wlo,
    loaded, stored, u_send, u_recv, m_send, m_recv, c_send, c_recv, p_send, p_recv,
):
    width, rows = src.shape
    nrel = rel.shape[0]
    chunks = blocks * BLOCK // CHUNK
    per = CHUNK // BLOCK
    slots = pay.shape[1]
    nt = ((1,), (1,))
    d = lax.axis_index("dom")
    s = lax.axis_index("serve")
    right, left = lax.rem(d + 1, dom), lax.rem(d + dom - 1, dom)
    peers = [lax.rem(s + j, serve) for j in range(1, serve)]

    loads = {}
    for i, (name, given, held) in enumerate((
        ("tgt", tgt_in, tgt), ("tst", tst_in, tst), ("shard", shard_in, shard),
        ("changed", changed_in, changed), ("rel", rel_in, rel), ("rid", rid_in, rid),
        ("src", src_in, src), ("sid", sid_in, sid), ("sst", sst_in, sst), ("tid", tid_in, tid),
        ("nb", nb_in, nb), ("cnt", cnt_in, cnt),
    )):
        loads[name] = pltpu.make_async_copy(given, held, loaded.at[i])
        loads[name].start()

    def arrived(*names):
        for name in names:
            loads[name].wait()

    barrier = pltpu.get_barrier_semaphore()
    for neighbour in (left, right):
        pl.semaphore_signal(barrier, inc=1, device_id=(neighbour, s), device_id_type=MESH)
    for peer in peers:
        pl.semaphore_signal(barrier, inc=1, device_id=(d, peer), device_id_type=MESH)

    eight = lax.broadcasted_iota(jnp.int32, (8, BLOCK), 0)
    halves = rows // BLOCK

    def pack(step, h, target, state):
        wire[step, h], most = to_wire(target)
        msend[step, h] = jnp.where(eight == 0, state, most)

    arrived("tgt", "tst")
    for h in range(halves):
        at = slice(h * BLOCK, (h + 1) * BLOCK)
        pack(0, h, tgt[:, at], tst[:, at])
    arrived("shard", "changed")
    code[...] = jnp.broadcast_to(
        jnp.where(changed[...] == 1, shard[...], -1).astype(F32), (8, rows)
    )
    pl.semaphore_wait(barrier, 2 + serve - 1)

    def ring(step, h):
        i = step * halves + h
        u = pltpu.make_async_remote_copy(
            src_ref=wire.at[step, h], dst_ref=ubuf.at[step, h], send_sem=u_send.at[i],
            recv_sem=u_recv.at[i], device_id=(right, s), device_id_type=MESH)
        m = pltpu.make_async_remote_copy(
            src_ref=msend.at[step, h], dst_ref=mbuf.at[step, h], send_sem=m_send.at[i],
            recv_sem=m_recv.at[i], device_id=(right, s), device_id_type=MESH)
        u.start()
        m.start()
        return u, m

    moving = [ring(0, h) for h in range(halves)]
    code_copies = []
    for j, peer in enumerate(peers):
        c = pltpu.make_async_remote_copy(
            src_ref=code, dst_ref=code_in.at[j], send_sem=c_send.at[j],
            recv_sem=c_recv.at[j], device_id=(d, peer), device_id_type=MESH)
        c.start()
        code_copies.append(c)

    row_of = lax.broadcasted_iota(jnp.int32, (rows, CHUNK), 0)
    edge = lax.broadcasted_iota(jnp.int32, (1, CHUNK), 1)

    def ids(ref, step, c):
        return jnp.concatenate(
            [ref[step, c * per + i : c * per + i + 1, :] for i in range(per)], axis=1)

    def one_hot(ref, step, c):
        return row_of == ids(ref, step, c)

    def ones(mask):
        return jnp.where(mask, 1.0, 0.0).astype(BF16)

    def per_edge(ref, step, c, offset):
        return jnp.concatenate([
            jnp.broadcast_to(ref[step : step + 1, c * per + i : c * per + i + 1], (1, BLOCK))
            + i * offset
            for i in range(per)
        ], axis=1)

    arrived("rel", "rid")
    parts, rest = [], rel[...]
    for i in range(3):
        parts.append(rest.astype(BF16).astype(F32))
        rest = rest - parts[-1]
    parts.append(jnp.zeros((BLOCK - 3 * nrel, width), F32))
    table = jnp.concatenate(parts, axis=0).T.astype(BF16)
    sub = lax.broadcasted_iota(jnp.int32, (BLOCK, CHUNK), 0)
    rel_of = jnp.where(sub < 3 * nrel, lax.rem(sub, nrel), -1)

    def relations(step):
        for c in range(chunks):
            at = (step * chunks + c) * CHUNK
            relg[:, at : at + CHUNK] = dot(table, ones(rel_of == ids(rid, step, c)))

    def queries(step, source):
        high, low = split(source)
        for c in range(chunks):
            hot = ones(one_hot(sid, step, c))
            at = (step * chunks + c) * CHUNK
            q = (dot(high, hot) + dot(low, hot)) * relg[:, at : at + CHUNK]
            q_high, q_low = split(q)
            qhi[:, c * CHUNK : (c + 1) * CHUNK] = q_high
            qlo[:, c * CHUNK : (c + 1) * CHUNK] = q_low

    def weights(step, h, target):
        high, low = split(target.T)
        for c in range(chunks):
            at = slice(c * CHUNK, (c + 1) * CHUNK)
            a, b = qhi[:, at], qlo[:, at]
            logits = dot(high, a) + dot(low, a) + dot(high, b)
            hot = row_of[:BLOCK] == ids(tid, step, c) - h * BLOCK
            valid = jnp.where(edge < per_edge(cnt, step, c, BLOCK), 1.0, 0.0)
            pos = jnp.sum(jnp.where(hot, logits, 0.0), axis=0, keepdims=True)
            dpos = -jax.nn.sigmoid(-pos) * valid
            share = jnp.where(per_edge(nb, step, c, 0) == h, valid / BLOCK, 0.0)
            w = jnp.where(hot, dpos, 0.0) + jax.nn.sigmoid(logits) * share
            w_high, w_low = split(w)
            whi[h * BLOCK : (h + 1) * BLOCK, at] = w_high
            wlo[h * BLOCK : (h + 1) * BLOCK, at] = w_low

    def target_grad(first, last):
        total = jnp.zeros((width, last - first), F32)
        for c in range(chunks):
            at = slice(c * CHUNK, (c + 1) * CHUNK)
            total += dot(qhi[:, at], whi[first:last, at], nt)
            total += dot(qlo[:, at], whi[first:last, at], nt)
            total += dot(qhi[:, at], wlo[first:last, at], nt)
        return total

    def source_grad(step, target):
        high, low = split(target)
        total = jnp.zeros((width, rows), F32)
        for c in range(chunks):
            at = slice(c * CHUNK, (c + 1) * CHUNK)
            g = dot(high, whi[:, at]) + dot(low, whi[:, at]) + dot(high, wlo[:, at])
            r = (step * chunks + c) * CHUNK
            g_high, g_low = split(g * relg[:, r : r + CHUNK])
            hot = ones(one_hot(sid, step, c))
            total += dot(g_high, hot, nt) + dot(g_low, hot, nt)
        return total

    def compaction(code_row, which):
        sel = jnp.where(code_row == which.astype(F32), 1.0, 0.0)
        before = lax.broadcasted_iota(jnp.int32, (rows, rows), 0)
        after = lax.broadcasted_iota(jnp.int32, (rows, rows), 1)
        rank = dot(jnp.broadcast_to(sel, (16, rows)).astype(BF16), ones(before < after))[:1, :]
        slot = lax.broadcasted_iota(jnp.int32, (slots, rows), 0).astype(F32)
        return ones((rank == slot) & (sel > 0.0))

    for step in range(steps):
        relations(step)
    arrived("src", "sid")
    source = src[...]
    queries(0, source)
    arrived("sst", "tid", "nb", "cnt")
    source_state = sst[...]
    own[...] = jnp.where(code[:1, :] == s.astype(F32), 1.0, 0.0)
    for j, peer in enumerate(peers):
        pick[j] = compaction(code[:1, :], peer)
    for j in range(serve - 1):
        code_copies[j].wait()
        expand[j] = compaction(code_in[j, :1, :], s)

    stores = []

    def store(*pairs):
        for held, out in pairs:
            copy = pltpu.make_async_copy(held, out, stored.at[len(stores)])
            copy.start()
            stores.append(copy)

    store((expand, o_expand), (own, o_code))
    for step in range(steps):
        last = step == steps - 1
        targets, states, later = [], [], []
        for h in range(halves):
            for copy in moving[h]:
                copy.wait()
            target = from_wire(ubuf[step, h], mbuf[step, h, 1:2, :])
            state = mbuf[step, h, :1, :]
            weights(step, h, target)
            targets.append(target)
            states.append(state)
            if not last:
                grad = target_grad(h * BLOCK, (h + 1) * BLOCK)
                target, state = adagrad(target, state, grad)
                pack(step + 1, h, target, state)
                later.append(ring(step + 1, h))
        moving = later
        old, target_state = jnp.concatenate(targets, axis=1), jnp.concatenate(states, axis=1)
        if not last:
            source, source_state = adagrad(source, source_state, source_grad(step, old))
            queries(step + 1, source)
        else:
            source, source_state = adagrad(source, source_state, source_grad(step, old))
            published = source.astype(BF16)
            pay_copies = []
            for j, peer in enumerate(peers):
                pay[j] = dot(pick[j], published, nt).astype(BF16)
                p = pltpu.make_async_remote_copy(
                    src_ref=pay.at[j], dst_ref=pay_in.at[j], send_sem=p_send.at[j],
                    recv_sem=p_recv.at[j], device_id=(d, peer), device_id_type=MESH)
                p.start()
                pay_copies.append(p)
            new_src[...] = source
            new_sst[...] = source_state
            store((new_src, o_src), (new_sst, o_sst))
            target, target_state = adagrad(old, target_state, target_grad(0, rows))
            new_tgt[...] = target
            new_tst[...] = target_state
            store((new_tgt, o_tgt), (new_tst, o_tst))
            for j in range(serve - 1):
                pay_copies[j].wait()
            store((pay_in, o_pay))
            for copy in stores:
                copy.wait()


def finish(serve, *refs):
    given, outs, held = refs[:7], refs[7:11], refs[12:19]
    o_served, served, loaded, stored, served_sems = refs[11], *refs[19:]
    src, _, _, _, pay, expand, own = held
    order = (4, 5, 0, 6, 2, 1, 3)
    loads = {i: pltpu.make_async_copy(given[i], held[i], loaded.at[i]) for i in order}
    for i in order:
        loads[i].start()
    copies = []

    def store(value, out, sem):
        copies.append(pltpu.make_async_copy(value, out, sem))
        copies[-1].start()

    s = lax.axis_index("serve")
    loads[4].wait()
    loads[5].wait()
    for j in range(1, serve + 1):
        if j == serve:
            for i in order[2:]:
                loads[i].wait()
                if i < 4:
                    store(held[i], outs[i], stored.at[i])
            piece = jnp.where(own[...] > 0.0, src[...], 0.0)
        else:
            piece = dot(pay[j - 1], expand[j - 1], ((0,), (0,)))
        served[j - 1] = piece.astype(BF16)
        sender = lax.rem(s + serve - j, serve)
        store(served.at[j - 1], o_served.at[sender], served_sems.at[j - 1])
    for copy in copies:
        copy.wait()


def on_device(
    dom, serve,
    source_rows, source_state, target_rows, target_state, relation_table,
    source_ids, target_ids, relation_ids, negative_block, edge_counts,
    serving_shard, changed_rows,
):
    _, _, rows, width = source_rows.shape
    _, _, steps, blocks, _ = source_ids.shape
    nrel = relation_table.shape[0]
    slots = rows // 4
    edges = blocks * BLOCK
    halves = rows // BLOCK
    moves = steps * halves
    hbm = pl.BlockSpec(memory_space=pltpu.HBM)
    dma = pltpu.SemaphoreType.DMA
    args = (
        source_rows[0, 0].T, source_state[0], target_rows[0, 0].T, target_state[0],
        relation_table, source_ids[0, 0], target_ids[0, 0], relation_ids[0, 0],
        negative_block[0, 0], edge_counts[0, 0], serving_shard[0], changed_rows[0],
    )
    state = (
        jax.ShapeDtypeStruct((width, rows), F32),
        jax.ShapeDtypeStruct((1, rows), F32),
        jax.ShapeDtypeStruct((width, rows), F32),
        jax.ShapeDtypeStruct((1, rows), F32),
    )
    handed = state + (
        jax.ShapeDtypeStruct((serve - 1, slots, width), BF16),
        jax.ShapeDtypeStruct((serve - 1, slots, rows), BF16),
        jax.ShapeDtypeStruct((1, rows), F32),
    )
    outs = pl.pallas_call(
        functools.partial(kernel, dom, serve, steps, blocks),
        out_shape=handed,
        in_specs=[hbm] * len(args),
        out_specs=(hbm,) * len(handed),
        scratch_shapes=[
            pltpu.VMEM(held.shape, held.dtype) for held in state + handed[5:] + args
        ] + [
            pltpu.VMEM((steps, halves, width, BLOCK), jnp.int16),
            pltpu.VMEM((steps, halves, width, BLOCK), jnp.int16),
            pltpu.VMEM((steps, halves, 8, BLOCK), F32),
            pltpu.VMEM((steps, halves, 8, BLOCK), F32),
            pltpu.VMEM((8, rows), F32),
            pltpu.VMEM((serve - 1, 8, rows), F32),
            pltpu.VMEM((serve - 1, slots, width), BF16),
            pltpu.VMEM((serve - 1, slots, width), BF16),
            pltpu.VMEM((serve - 1, slots, rows), BF16),
            pltpu.VMEM((width, steps * edges), F32),
            pltpu.VMEM((width, edges), BF16),
            pltpu.VMEM((width, edges), BF16),
            pltpu.VMEM((rows, edges), BF16),
            pltpu.VMEM((rows, edges), BF16),
            dma((len(args),)), dma((len(handed),)),
            dma((moves,)), dma((moves,)), dma((moves,)), dma((moves,)),
            dma((serve - 1,)), dma((serve - 1,)), dma((serve - 1,)), dma((serve - 1,)),
        ],
        compiler_params=pltpu.CompilerParams(
            collective_id=0, has_side_effects=True, vmem_limit_bytes=60 * 1024 * 1024
        ),
        name="train",
    )(*args)
    source, source_sums, target, target_sums, served = pl.pallas_call(
        functools.partial(finish, serve),
        out_shape=state + (jax.ShapeDtypeStruct((serve, width, rows), BF16),),
        in_specs=[hbm] * len(handed),
        out_specs=(hbm,) * 5,
        scratch_shapes=[pltpu.VMEM(held.shape, held.dtype) for held in handed] + [
            pltpu.VMEM((serve, width, rows), BF16),
            dma((len(handed),)), dma((4,)), dma((serve,)),
        ],
        compiler_params=pltpu.CompilerParams(vmem_limit_bytes=60 * 1024 * 1024),
        name="publish",
    )(*outs)
    return (source.T[None, None], source_sums[None], target.T[None, None], target_sums[None],
            jnp.swapaxes(served, 1, 2)[None, None])


def solution(mesh):
    rows4 = P("dom", "serve", None, None)
    rows3 = P("dom", "serve", None)
    ids = P("dom", "serve", None, None, None)
    return jax.shard_map(
        functools.partial(on_device, mesh.shape["dom"], mesh.shape["serve"]),
        mesh=mesh,
        in_specs=(rows4, rows3, rows4, rows3, P(), ids, ids, ids, rows4, rows4, rows3, rows3),
        out_specs=(rows4, rows3, rows4, rows3, ids),
        check_vma=False,
    )
```

```python
import functools
import jax
import jax.numpy as jnp
from jax import lax
from jax.experimental import pallas as pl
from jax.experimental.pallas import tpu as pltpu
from jax.sharding import PartitionSpec as P

LEARN_RATE = 0.1
EPSILON = 1e-08
BLOCK = 128
CHUNK = 256
WIRE_MAX = 32767.0
TINY = 1e-30
MESH = pl.DeviceIdType.MESH
F32 = jnp.float32
BF16 = jnp.bfloat16


def dot(a, b, contract=((1,), (0,))):
    return lax.dot_general(a, b, (contract, ((), ())), preferred_element_type=F32)


def split(x):
    high = x.astype(BF16)
    return high, (x - high.astype(F32)).astype(BF16)


def to_wire(u):
    most = jnp.maximum(jnp.max(jnp.abs(u), axis=0, keepdims=True), TINY)
    return jnp.floor(u * (WIRE_MAX / most) + 0.5).astype(jnp.int32).astype(jnp.int16), most


def stacked(x):
    return jnp.concatenate(split(x), axis=0)


def halves_sum(x):
    n = x.shape[0] // 2
    return x[:n] + x[n:]


def from_wire(q, most):
    return q.astype(jnp.int32).astype(F32) * (most * (1.0 / WIRE_MAX))


def adagrad(weights, state, grad):
    state = state + jnp.mean(grad * grad, axis=0, keepdims=True)
    rate = LEARN_RATE / (jnp.sqrt(state) + EPSILON)
    return weights - rate * grad, state


def kernel(
    dom, serve, steps, blocks,
    src_in, sst_in, tgt_in, tst_in, rel_in, sid_in, tid_in, rid_in, nb_in, cnt_in, shard_in,
    changed_in,
    o_src, o_sst, o_tgt, o_tst, o_pay, o_expand, o_code,
    new_src, new_sst, new_tgt, new_tst, expand, own,
    src, sst, tgt, tst, rel, sid, tid, rid, nb, cnt, shard, changed,
    ubuf, wire, mbuf, msend, code, code_in, pay, pay_in, pick,
    relg, hots, q_parts, g_parts, whi, wlo,
    loaded, stored, u_send, u_recv, m_send, m_recv, c_send, c_recv, p_send, p_recv,
):
    width, rows = src.shape
    nrel = rel.shape[0]
    chunks = blocks * BLOCK // CHUNK
    per = CHUNK // BLOCK
    slots = pay.shape[1]
    nt = ((1,), (1,))
    d = lax.axis_index("dom")
    s = lax.axis_index("serve")
    right, left = lax.rem(d + 1, dom), lax.rem(d + dom - 1, dom)
    peers = [lax.rem(s + j, serve) for j in range(1, serve)]

    barrier = pltpu.get_barrier_semaphore()
    for neighbour in (left, right):
        pl.semaphore_signal(barrier, inc=1, device_id=(neighbour, s), device_id_type=MESH)
    for peer in peers:
        pl.semaphore_signal(barrier, inc=1, device_id=(d, peer), device_id_type=MESH)

    loads = {}
    for i, (name, given, held) in enumerate((
        ("tgt", tgt_in, tgt), ("tst", tst_in, tst), ("shard", shard_in, shard),
        ("changed", changed_in, changed), ("rel", rel_in, rel), ("rid", rid_in, rid),
        ("src", src_in, src), ("sid", sid_in, sid), ("sst", sst_in, sst), ("tid", tid_in, tid),
        ("nb", nb_in, nb), ("cnt", cnt_in, cnt),
    )):
        loads[name] = pltpu.make_async_copy(given, held, loaded.at[i])
        loads[name].start()

    def arrived(*names):
        for name in names:
            loads[name].wait()

    eight = lax.broadcasted_iota(jnp.int32, (8, BLOCK), 0)
    halves = rows // BLOCK

    def pack(step, h, target, state):
        wire[step, h], most = to_wire(target)
        msend[step, h] = jnp.where(eight == 0, state, most)

    arrived("tgt", "tst")
    for h in range(halves):
        at = slice(h * BLOCK, (h + 1) * BLOCK)
        pack(0, h, tgt[:, at], tst[:, at])
    arrived("shard", "changed")
    code[...] = jnp.broadcast_to(
        jnp.where(changed[...] == 1, shard[...], -1).astype(F32), (8, rows)
    )
    pl.semaphore_wait(barrier, 2 + serve - 1)

    def ring(step, h):
        i = step * halves + h
        u = pltpu.make_async_remote_copy(
            src_ref=wire.at[step, h], dst_ref=ubuf.at[step, h], send_sem=u_send.at[i],
            recv_sem=u_recv.at[i], device_id=(right, s), device_id_type=MESH)
        m = pltpu.make_async_remote_copy(
            src_ref=msend.at[step, h], dst_ref=mbuf.at[step, h], send_sem=m_send.at[i],
            recv_sem=m_recv.at[i], device_id=(right, s), device_id_type=MESH)
        u.start()
        m.start()
        return u, m

    moving = [ring(0, h) for h in range(halves)]
    code_copies = []
    for j, peer in enumerate(peers):
        c = pltpu.make_async_remote_copy(
            src_ref=code, dst_ref=code_in.at[j], send_sem=c_send.at[j],
            recv_sem=c_recv.at[j], device_id=(d, peer), device_id_type=MESH)
        c.start()
        code_copies.append(c)

    row_of = lax.broadcasted_iota(jnp.int32, (rows, CHUNK), 0)
    edge = lax.broadcasted_iota(jnp.int32, (1, CHUNK), 1)

    def ids(ref, step, c):
        return jnp.concatenate(
            [ref[step, c * per + i : c * per + i + 1, :] for i in range(per)], axis=1)

    def one_hot(ref, step, c):
        return row_of == ids(ref, step, c)

    def ones(mask):
        return jnp.where(mask, 1.0, 0.0).astype(BF16)

    def per_edge(ref, step, c, offset):
        return jnp.concatenate([
            jnp.broadcast_to(ref[step : step + 1, c * per + i : c * per + i + 1], (1, BLOCK))
            + i * offset
            for i in range(per)
        ], axis=1)

    arrived("rel", "rid")
    parts, rest = [], rel[...]
    for i in range(3):
        parts.append(rest.astype(BF16).astype(F32))
        rest = rest - parts[-1]
    parts.append(jnp.zeros((BLOCK - 3 * nrel, width), F32))
    table = jnp.concatenate(parts, axis=0).T.astype(BF16)
    sub = lax.broadcasted_iota(jnp.int32, (BLOCK, CHUNK), 0)
    rel_of = jnp.where(sub < 3 * nrel, lax.rem(sub, nrel), -1)

    def relations(step):
        for c in range(chunks):
            at = (step * chunks + c) * CHUNK
            relg[:, at : at + CHUNK] = dot(table, ones(rel_of == ids(rid, step, c)))

    def queries(step, source):
        both = stacked(source)
        for c in range(chunks):
            hot = ones(one_hot(sid, step, c))
            at = (step * chunks + c) * CHUNK
            q_high, q_low = split(halves_sum(dot(both, hot)) * relg[:, at : at + CHUNK])
            at = slice(c * CHUNK, (c + 1) * CHUNK)
            hots[:, at] = hot
            q_parts[:width, at] = q_high
            q_parts[width:, at] = q_low

    def weights(step, h, target):
        both = stacked(target.T)
        for c in range(chunks):
            at = slice(c * CHUNK, (c + 1) * CHUNK)
            logits = halves_sum(dot(both, q_parts[:width, at]))
            logits += dot(both[:BLOCK], q_parts[width:, at])
            hot = row_of[:BLOCK] == ids(tid, step, c) - h * BLOCK
            valid = jnp.where(edge < per_edge(cnt, step, c, BLOCK), 1.0, 0.0)
            pos = jnp.sum(jnp.where(hot, logits, 0.0), axis=0, keepdims=True)
            dpos = -jax.nn.sigmoid(-pos) * valid
            share = jnp.where(per_edge(nb, step, c, 0) == h, valid * (0.5 / BLOCK), 0.0)
            w = jnp.where(hot, dpos + share, share) + jnp.tanh(0.5 * logits) * share
            w_high, w_low = split(w)
            whi[h * BLOCK : (h + 1) * BLOCK, at] = w_high
            wlo[h * BLOCK : (h + 1) * BLOCK, at] = w_low

    def target_grad(first, last):
        total = halves_sum(dot(q_parts[...], whi[first:last, :], nt))
        return total + dot(q_parts[:width, :], wlo[first:last, :], nt)

    def source_grad(step, target):
        both = stacked(target)
        for c in range(chunks):
            at = slice(c * CHUNK, (c + 1) * CHUNK)
            g = halves_sum(dot(both, whi[:, at])) + dot(both[:width], wlo[:, at])
            r = (step * chunks + c) * CHUNK
            g_high, g_low = split(g * relg[:, r : r + CHUNK])
            g_parts[:width, at] = g_high
            g_parts[width:, at] = g_low
        return halves_sum(dot(g_parts[...], hots[...], nt))

    def compaction(code_row, which):
        sel = jnp.where(code_row == which.astype(F32), 1.0, 0.0)
        before = lax.broadcasted_iota(jnp.int32, (rows, rows), 0)
        after = lax.broadcasted_iota(jnp.int32, (rows, rows), 1)
        rank = dot(jnp.broadcast_to(sel, (16, rows)).astype(BF16), ones(before < after))[:1, :]
        slot = lax.broadcasted_iota(jnp.int32, (slots, rows), 0).astype(F32)
        return ones((rank == slot) & (sel > 0.0))

    for step in range(steps):
        relations(step)
    arrived("src", "sid")
    source = src[...]
    queries(0, source)
    arrived("sst", "tid", "nb", "cnt")
    source_state = sst[...]
    own[...] = jnp.where(code[:1, :] == s.astype(F32), 1.0, 0.0)
    for j, peer in enumerate(peers):
        pick[j] = compaction(code[:1, :], peer)
    for j in range(serve - 1):
        code_copies[j].wait()
        expand[j] = compaction(code_in[j, :1, :], s)

    stores = []

    def store(*pairs):
        for held, out in pairs:
            copy = pltpu.make_async_copy(held, out, stored.at[len(stores)])
            copy.start()
            stores.append(copy)

    store((expand, o_expand), (own, o_code))
    for step in range(steps):
        last = step == steps - 1
        targets, states, later = [], [], []
        for h in range(halves):
            for copy in moving[h]:
                copy.wait()
            target = from_wire(ubuf[step, h], mbuf[step, h, 1:2, :])
            state = mbuf[step, h, :1, :]
            weights(step, h, target)
            targets.append(target)
            states.append(state)
            if not last:
                grad = target_grad(h * BLOCK, (h + 1) * BLOCK)
                target, state = adagrad(target, state, grad)
                pack(step + 1, h, target, state)
                later.append(ring(step + 1, h))
        moving = later
        old, target_state = jnp.concatenate(targets, axis=1), jnp.concatenate(states, axis=1)
        if not last:
            source, source_state = adagrad(source, source_state, source_grad(step, old))
            queries(step + 1, source)
        else:
            source, source_state = adagrad(source, source_state, source_grad(step, old))
            published = source.astype(BF16)
            pay_copies = []
            for j, peer in enumerate(peers):
                pay[j] = dot(pick[j], published, nt).astype(BF16)
                p = pltpu.make_async_remote_copy(
                    src_ref=pay.at[j], dst_ref=pay_in.at[j], send_sem=p_send.at[j],
                    recv_sem=p_recv.at[j], device_id=(d, peer), device_id_type=MESH)
                p.start()
                pay_copies.append(p)
            new_src[...] = source
            new_sst[...] = source_state
            store((new_src, o_src), (new_sst, o_sst))
            target, target_state = adagrad(old, target_state, target_grad(0, rows))
            new_tgt[...] = target
            new_tst[...] = target_state
            store((new_tgt, o_tgt), (new_tst, o_tst))
            for j in range(serve - 1):
                pay_copies[j].wait()
            store((pay_in, o_pay))
            for copy in stores:
                copy.wait()


def finish(serve, *refs):
    given, outs, held = refs[:7], refs[7:11], refs[12:19]
    o_served, served, loaded, stored, served_sems = refs[11], *refs[19:]
    src, _, _, _, pay, expand, own = held
    order = (4, 5, 0, 6, 2, 1, 3)
    loads = {i: pltpu.make_async_copy(given[i], held[i], loaded.at[i]) for i in order}
    for i in order:
        loads[i].start()
    copies = []

    def store(value, out, sem):
        copies.append(pltpu.make_async_copy(value, out, sem))
        copies[-1].start()

    s = lax.axis_index("serve")
    loads[4].wait()
    loads[5].wait()
    for j in range(1, serve + 1):
        if j == serve:
            for i in order[2:]:
                loads[i].wait()
                if i < 4:
                    store(held[i], outs[i], stored.at[i])
            piece = jnp.where(own[...] > 0.0, src[...], 0.0)
        else:
            piece = dot(pay[j - 1], expand[j - 1], ((0,), (0,)))
        served[j - 1] = piece.astype(BF16)
        sender = lax.rem(s + serve - j, serve)
        store(served.at[j - 1], o_served.at[sender], served_sems.at[j - 1])
    for copy in copies:
        copy.wait()


def on_device(
    dom, serve,
    source_rows, source_state, target_rows, target_state, relation_table,
    source_ids, target_ids, relation_ids, negative_block, edge_counts,
    serving_shard, changed_rows,
):
    _, _, rows, width = source_rows.shape
    _, _, steps, blocks, _ = source_ids.shape
    nrel = relation_table.shape[0]
    slots = rows // 4
    edges = blocks * BLOCK
    halves = rows // BLOCK
    moves = steps * halves
    hbm = pl.BlockSpec(memory_space=pltpu.HBM)
    dma = pltpu.SemaphoreType.DMA
    args = (
        source_rows[0, 0].T, source_state[0], target_rows[0, 0].T, target_state[0],
        relation_table, source_ids[0, 0], target_ids[0, 0], relation_ids[0, 0],
        negative_block[0, 0], edge_counts[0, 0], serving_shard[0], changed_rows[0],
    )
    state = (
        jax.ShapeDtypeStruct((width, rows), F32),
        jax.ShapeDtypeStruct((1, rows), F32),
        jax.ShapeDtypeStruct((width, rows), F32),
        jax.ShapeDtypeStruct((1, rows), F32),
    )
    handed = state + (
        jax.ShapeDtypeStruct((serve - 1, slots, width), BF16),
        jax.ShapeDtypeStruct((serve - 1, slots, rows), BF16),
        jax.ShapeDtypeStruct((1, rows), F32),
    )
    outs = pl.pallas_call(
        functools.partial(kernel, dom, serve, steps, blocks),
        out_shape=handed,
        in_specs=[hbm] * len(args),
        out_specs=(hbm,) * len(handed),
        scratch_shapes=[
            pltpu.VMEM(held.shape, held.dtype) for held in state + handed[5:] + args
        ] + [
            pltpu.VMEM((steps, halves, width, BLOCK), jnp.int16),
            pltpu.VMEM((steps, halves, width, BLOCK), jnp.int16),
            pltpu.VMEM((steps, halves, 8, BLOCK), F32),
            pltpu.VMEM((steps, halves, 8, BLOCK), F32),
            pltpu.VMEM((8, rows), F32),
            pltpu.VMEM((serve - 1, 8, rows), F32),
            pltpu.VMEM((serve - 1, slots, width), BF16),
            pltpu.VMEM((serve - 1, slots, width), BF16),
            pltpu.VMEM((serve - 1, slots, rows), BF16),
            pltpu.VMEM((width, steps * edges), F32),
            pltpu.VMEM((rows, edges), BF16),
            pltpu.VMEM((2 * width, edges), BF16),
            pltpu.VMEM((2 * width, edges), BF16),
            pltpu.VMEM((rows, edges), BF16),
            pltpu.VMEM((rows, edges), BF16),
            dma((len(args),)), dma((len(handed),)),
            dma((moves,)), dma((moves,)), dma((moves,)), dma((moves,)),
            dma((serve - 1,)), dma((serve - 1,)), dma((serve - 1,)), dma((serve - 1,)),
        ],
        compiler_params=pltpu.CompilerParams(
            collective_id=0, has_side_effects=True, vmem_limit_bytes=60 * 1024 * 1024
        ),
        name="train",
    )(*args)
    source, source_sums, target, target_sums, served = pl.pallas_call(
        functools.partial(finish, serve),
        out_shape=state + (jax.ShapeDtypeStruct((serve, width, rows), BF16),),
        in_specs=[hbm] * len(handed),
        out_specs=(hbm,) * 5,
        scratch_shapes=[pltpu.VMEM(held.shape, held.dtype) for held in handed] + [
            pltpu.VMEM((serve, width, rows), BF16),
            dma((len(handed),)), dma((4,)), dma((serve,)),
        ],
        compiler_params=pltpu.CompilerParams(vmem_limit_bytes=60 * 1024 * 1024),
        name="publish",
    )(*outs)
    return (source.T[None, None], source_sums[None], target.T[None, None], target_sums[None],
            jnp.swapaxes(served, 1, 2)[None, None])


def solution(mesh):
    rows4 = P("dom", "serve", None, None)
    rows3 = P("dom", "serve", None)
    ids = P("dom", "serve", None, None, None)
    return jax.shard_map(
        functools.partial(on_device, mesh.shape["dom"], mesh.shape["serve"]),
        mesh=mesh,
        in_specs=(rows4, rows3, rows4, rows3, P(), ids, ids, ids, rows4, rows4, rows3, rows3),
        out_specs=(rows4, rows3, rows4, rows3, ids),
        check_vma=False,
    )
```
